32 devices in a mesh: dom: 16 (over z, y, core), tile: 2 (over x).
Axes of the slice: x: 2, y: 2, z: 4, core: 2. Of those that a mesh axis runs over, the one named last changes fastest.
Arguments:
- states: float32 [16, 3, 128, 2048], P('dom', None, 'tile'), may hold values from -6 to 6
- offspring: int32 [16], replicated, may hold values from 0 to 4, as said below
- sea_depth: float32 [128, 2048], P('tile'), may hold values from 0.5 to 2
- wind: bfloat16 [6, 2, 64, 1024], P('tile'), may hold values from -6 to 6
- start_hour: int32 [1], replicated, may hold values from 0 to 4
Outputs:
- new_states: float32 [16, 3, 128, 2048], P('dom', None, 'tile')
The draws below stay inside these ranges and needn't reach their ends.
Inputs may be any that keep to these rules, and one draw needn't show every extreme that they name: offspring counts are whole numbers that sum to 16. The step runs from hour start_hour[0] to the next hour.
All inputs are finite; a program needn't handle non-finite values.
Results may differ from the reference program's by a relative error of at most 0.001.
Values may be sent and summed in bfloat16 or wider, within the bound.
No kernel may reach another device: no remote copies, remote signals or barrier semaphores. Data moves between devices by JAX's collectives and lax.ppermute only.
A program may use at most 128 MiB of HBM per device.

```python
import math
import jax
import jax.numpy as jnp
from jax import lax

COLS = 2048
PARTICLES = 16
NROWS = 128
HOURS = 6


def draw_offspring(key, part):
    cut_key, perm_key = jax.random.split(jax.random.fold_in(key, 17))
    groups = PARTICLES // 4
    cuts = jnp.sort(jax.random.randint(cut_key, (groups, 3), 0, 5, dtype=jnp.int32), axis=1)
    lower = jnp.concatenate([jnp.zeros((groups, 1), jnp.int32), cuts], axis=1)
    upper = jnp.concatenate([cuts, jnp.full((groups, 1), 4, jnp.int32)], axis=1)
    counts = (upper - lower).astype(jnp.int32)
    fixed = jnp.array([4, 0, 0, 0], dtype=jnp.int32)
    counts = counts.at[0].set(fixed)
    order = jax.random.permutation(perm_key, PARTICLES)
    flat = counts.reshape(PARTICLES)
    return jnp.zeros((PARTICLES,), jnp.int32).at[order].set(flat).astype(jnp.int32)


def block_scale(stream_key, shape, cuts, smallest, high):
    gain = 1.0
    for position, shards_of in cuts:
        steps = jax.random.uniform(jax.random.fold_in(jax.random.fold_in(stream_key, 6), position), (shards_of,), jnp.float32, smallest / len(cuts), high / len(cuts))
        gain = gain * jnp.repeat(jnp.exp(steps), shape[position] // shards_of).reshape((-1,) + (1,) * (len(shape) - 1 - position))
    return gain


def centred(stream_key, extent, width, most, cuts=(), held_as=jnp.bfloat16):
    level = block_scale(stream_key, extent, cuts, -0.22, 0.18) if cuts else 1.0
    drawn = jax.random.normal(stream_key, extent, jnp.float32) * width * level
    return jnp.minimum(jnp.maximum(drawn, -most), most).astype(held_as)


def setup_inputs(seed: int = 0) -> dict:
    splits = jax.random.split(jax.random.key(seed), 6)
    states = centred(splits[0], (PARTICLES, 3, NROWS, COLS), 1.0, 6.0, ((0, 16), (2, 2)), jnp.float32)
    offspring = draw_offspring(jax.random.fold_in(splits[5], 71), 0)
    sea_depth = jnp.clip(jnp.exp(math.log(2.0) - 1.3862944 * jax.random.uniform(splits[2], (NROWS, COLS), jnp.float32) ** block_scale(splits[2], (NROWS, COLS), ((0, 2),), -0.2, 0.2)), 0.5, 2.0)
    wind = centred(splits[3], (HOURS, 2, NROWS // 2, COLS // 2), 1.0, 6.0, ((0, 2),))
    start_hour = jax.random.randint(splits[4], (1,), 0, HOURS - 1).astype(jnp.int32)
    return dict(states=states, offspring=offspring, sea_depth=sea_depth, wind=wind, start_hour=start_hour)


GRAVITY = 1.0
FRICTION = 0.1
TIME_STEP = 0.4


def parent_list(offspring):
    count = offspring.shape[0]
    running = jnp.cumsum(offspring).astype(jnp.int32)
    slots = jnp.arange(count, dtype=jnp.int32)
    return jnp.sum((running[None, :] <= slots[:, None]).astype(jnp.int32), axis=1).astype(jnp.int32)


def along_cols(field):
    return (jnp.roll(field, -1, axis=-1) - jnp.roll(field, 1, axis=-1)) * 0.5


def along_rows(padded):
    return (padded[..., 2:, :] - padded[..., :-2, :]) * 0.5


def upsample(panel):
    return jnp.repeat(jnp.repeat(panel, 2, axis=-2), 2, axis=-1).astype(jnp.float32)


def spin_rate(global_rows, total_rows):
    return (0.1 + 0.4 * global_rows.astype(jnp.float32) / total_rows)[:, None]


def tendency(state, sea_depth, spin, stress):
    surface = state[0]
    eastward = state[1]
    northward = state[2]
    flux_east = sea_depth * eastward
    flux_north = sea_depth * northward
    pad_surface = jnp.pad(surface, ((1, 1), (0, 0)))
    pad_north = jnp.pad(flux_north, ((1, 1), (0, 0)))
    d_surface = -(along_cols(flux_east) + along_rows(pad_north))
    d_east = spin * northward - GRAVITY * along_cols(surface) + stress[0] - FRICTION * eastward
    d_north = -spin * eastward - GRAVITY * along_rows(pad_surface) + stress[1] - FRICTION * northward
    return jnp.stack([d_surface, d_east, d_north])


def reference(states, offspring, sea_depth, wind, start_hour):
    parents = parent_list(offspring)
    copied = jnp.take(states, parents, axis=0)
    first = start_hour[0]
    wind_now = upsample(lax.dynamic_index_in_dim(wind, first, 0, keepdims=False))
    wind_next = upsample(lax.dynamic_index_in_dim(wind, first + 1, 0, keepdims=False))
    wind_mid = 0.5 * (wind_now + wind_next)
    spin = spin_rate(jnp.arange(NROWS, dtype=jnp.int32), NROWS)

    def advance(state):
        section_one = state + TIME_STEP * tendency(state, sea_depth, spin, wind_now)
        section_two = 0.75 * state + 0.25 * (section_one + TIME_STEP * tendency(section_one, sea_depth, spin, wind_next))
        return (1.0 / 3.0) * state + (2.0 / 3.0) * (section_two + TIME_STEP * tendency(section_two, sea_depth, spin, wind_mid))

    return lax.map(advance, copied)
```

```python
import functools

import jax
import jax.numpy as jnp
from jax import lax
from jax.experimental import pallas as pl
from jax.experimental.pallas import tpu as pltpu
from jax.sharding import PartitionSpec as P

FRICTION = 0.1
TIME_STEP = 0.4
EDGE = 3
PAD = 8
VMEM_BYTES = 48 * 1024 * 1024


def parent_list(offspring):
    count = offspring.shape[0]
    running = jnp.cumsum(offspring)
    slots = jnp.arange(count, dtype=jnp.int32)
    return jnp.sum((running[None, :] <= slots[:, None]).astype(jnp.int32), axis=1)


def swap_edges(head, tail):
    count = lax.axis_size("tile")
    me = lax.axis_index("tile")
    above = jnp.zeros_like(head)
    below = jnp.zeros_like(head)
    for parity in range(2):
        pairs = []
        for i in range(parity, count - 1, 2):
            pairs += [(i, i + 1), (i + 1, i)]
        if pairs:
            upper = me % 2 == parity
            got = lax.ppermute(jnp.where(upper, tail, head), "tile", pairs)
            below = jnp.where(upper, got, below)
            above = jnp.where(upper, above, got)
    return above, below


def wind_window(wind, start_hour, row_count):
    count = lax.axis_size("tile")
    me = lax.axis_index("tile")
    hours_dev, parts, coarse_rows, coarse_cols = wind.shape
    own_rows = row_count // 2
    window = min(own_rows + 2 * PAD, coarse_rows)

    def first_row(tile):
        return jnp.clip(tile * own_rows - PAD, 0, coarse_rows - window)

    hours = [start_hour[0], start_hour[0] + 1]

    def panels(tile):
        return jnp.concatenate(
            [
                lax.dynamic_slice(
                    wind, (hour % hours_dev, 0, first_row(tile), 0), (1, parts, window, coarse_cols)
                )
                for hour in hours
            ]
        )

    owner = jnp.stack(hours)[:, None, None, None] // hours_dev
    found = panels(me)
    for shift in range(1, count):
        got = lax.ppermute(
            panels((me + shift) % count), "tile", [(i, (i + shift) % count) for i in range(count)]
        )
        found = jnp.where(owner == (me - shift) % count, got, found)
    return found, first_row(me)


def wind_kernel(where_ref, coarse_ref, fine_ref):
    hours, parts, window, coarse_cols = coarse_ref.shape
    rows = fine_ref.shape[2]
    first = where_ref[0]
    base = where_ref[1]
    fine_row = lax.broadcasted_iota(jnp.int32, (rows, window), 0) + first
    coarse_row = lax.broadcasted_iota(jnp.int32, (rows, window), 1) + base
    lift = jnp.where((fine_row >> 1) == coarse_row, 1.0, 0.0).astype(jnp.bfloat16)
    step = 128
    fine_col = lax.broadcasted_iota(jnp.int32, (step, 2 * step), 1)
    coarse_col = lax.broadcasted_iota(jnp.int32, (step, 2 * step), 0)
    widen = jnp.where((fine_col >> 1) == coarse_col, 1.0, 0.0).astype(jnp.bfloat16)
    for hour in range(hours):
        for part in range(parts):
            for left in range(0, coarse_cols, step):
                cells = coarse_ref[hour, part, :, left : left + step]
                wide = jnp.dot(cells, widen, preferred_element_type=jnp.float32)
                tall = jnp.dot(
                    lift, wide.astype(jnp.bfloat16), preferred_element_type=jnp.float32
                )
                fine_ref[hour, part, :, 2 * left : 2 * (left + step)] = TIME_STEP * tall


def fine_wind(coarse, first, base, rows):
    hours, parts, window, cols = coarse.shape
    return pl.pallas_call(
        wind_kernel,
        out_shape=jax.ShapeDtypeStruct((hours, parts, rows, 2 * cols), jnp.float32),
        in_specs=[
            pl.BlockSpec(memory_space=pltpu.SMEM),
            pl.BlockSpec(memory_space=pltpu.VMEM),
        ],
        out_specs=pl.BlockSpec(memory_space=pltpu.VMEM),
        compiler_params=pltpu.CompilerParams(vmem_limit_bytes=VMEM_BYTES),
        cost_estimate=pl.CostEstimate(
            flops=4 * hours * parts * rows * window * cols,
            bytes_accessed=8 * hours * parts * rows * cols,
            transcendentals=0,
        ),
    )(jnp.stack([first, base]).astype(jnp.int32), coarse)


def step_kernel(total_rows, where_ref, state_ref, depth_ref, wind_ref, out_ref, one, two, flux):
    rows = state_ref.shape[1]
    cols = state_ref.shape[2]
    blocks = rows // PAD
    first = where_ref[0]

    def shifted(ref, index, row, by):
        if 0 <= row + by <= rows - PAD:
            return ref[index, row + by : row + by + PAD, :]
        return pltpu.roll(ref[index, row : row + PAD, :], -by % PAD, 0)

    def across(field):
        return pltpu.roll(field, cols - 1, 1) - pltpu.roll(field, 1, 1)

    def section(source, stress, share, store, chosen):
        for block in range(blocks):
            low = block * PAD
            here = pl.ds(low, PAD)
            flux[0, here, :] = depth_ref[here, :] * source[2, here, :]
        for block in chosen:
            low = block * PAD
            here = pl.ds(low, PAD)
            row = first + low + lax.broadcasted_iota(jnp.int32, (PAD, 1), 0)
            turn = TIME_STEP * (0.1 + 0.4 * row.astype(jnp.float32) / total_rows)
            surface = source[0, here, :]
            east = source[1, here, :]
            north = source[2, here, :]
            flux_up = shifted(flux, 0, low, 1) - shifted(flux, 0, low, -1)
            next_surface = surface - (across(depth_ref[here, :] * east) + flux_up)
            rise = shifted(source, 0, low, 1) - shifted(source, 0, low, -1)
            half = 0.5 * TIME_STEP
            keep = 1.0 - TIME_STEP * FRICTION
            next_east = keep * east + turn * north - half * across(surface) + stress(0, here)
            next_north = keep * north - turn * east - half * rise + stress(1, here)
            inside = None
            if block == 0 or block == blocks - 1:
                inside = (row >= 0) & (row < total_rows)
            for part, value in enumerate((next_surface, next_east, next_north)):
                if share != 1.0:
                    value = (1.0 - share) * state_ref[part, here, :] + share * value
                if inside is not None:
                    value = jnp.where(inside, value, 0.0)
                store(part, low, value)

    def into(target):
        def store(part, low, value):
            target[part, pl.ds(low, PAD), :] = value

        return store

    def finish(part, low, value):
        out_ref[part, pl.ds(low - PAD, PAD), :] = value

    everything = range(blocks)
    section(state_ref, lambda part, here: wind_ref[0, part, here, :], 1.0, into(one), everything)
    section(one, lambda part, here: wind_ref[1, part, here, :], 0.25, into(two), everything)
    section(
        two,
        lambda part, here: 0.5 * (wind_ref[0, part, here, :] + wind_ref[1, part, here, :]),
        2.0 / 3.0,
        finish,
        range(1, blocks - 1),
    )


def step(state, depth, wind, first, total_rows):
    parts, rows, cols = state.shape
    own = rows - 2 * PAD
    vmem = pl.BlockSpec(memory_space=pltpu.VMEM)
    return pl.pallas_call(
        functools.partial(step_kernel, total_rows),
        out_shape=jax.ShapeDtypeStruct((parts, own, cols), jnp.float32),
        in_specs=[pl.BlockSpec(memory_space=pltpu.SMEM), vmem, vmem, vmem],
        out_specs=vmem,
        scratch_shapes=[
            pltpu.VMEM((parts, rows, cols), jnp.float32),
            pltpu.VMEM((parts, rows, cols), jnp.float32),
            pltpu.VMEM((1, rows, cols), jnp.float32),
        ],
        compiler_params=pltpu.CompilerParams(vmem_limit_bytes=VMEM_BYTES),
        cost_estimate=pl.CostEstimate(
            flops=100 * parts * rows * cols,
            bytes_accessed=4 * (3 * parts + 3) * rows * cols,
            transcendentals=0,
        ),
    )(first[None].astype(jnp.int32), state, depth, wind)


def exchange_all(cells, parents):
    spread = lax.all_to_all(cells, "dom", split_axis=3, concat_axis=0, tiled=True)
    picked = jnp.take(spread, parents, axis=0)
    return lax.all_to_all(picked, "dom", split_axis=0, concat_axis=3, tiled=True)


def body(states, offspring, sea_depth, wind, start_hour):
    row_count = states.shape[2]
    total_rows = row_count * lax.axis_size("tile")
    first = lax.axis_index("tile") * row_count - PAD
    parents = parent_list(offspring)
    coarse, base = wind_window(wind, start_hour, row_count)
    rows = row_count + 2 * PAD
    stress = fine_wind(coarse, first, base, rows)
    fill = ((PAD - EDGE, 0), (0, 0)), ((0, PAD - EDGE), (0, 0))

    depth_above, depth_below = swap_edges(sea_depth[:EDGE], sea_depth[-EDGE:])
    depth = (0.5 * TIME_STEP) * jnp.concatenate(
        [jnp.pad(depth_above, fill[0]), sea_depth, jnp.pad(depth_below, fill[1])]
    )
    copied = exchange_all(states.astype(jnp.float16), parents)[0]
    above, below = swap_edges(copied[:, :EDGE], copied[:, -EDGE:])
    state = jnp.concatenate(
        [
            jnp.pad(above, ((0, 0),) + fill[0]),
            copied,
            jnp.pad(below, ((0, 0),) + fill[1]),
        ],
        axis=1,
    ).astype(jnp.float32)
    return step(state, depth, stress, first, total_rows)[None]


def solution(mesh):
    return jax.shard_map(
        body,
        mesh=mesh,
        in_specs=(
            P("dom", None, "tile", None),
            P(),
            P("tile", None),
            P("tile", None, None, None),
            P(),
        ),
        out_specs=P("dom", None, "tile", None),
        check_vma=False,
    )
```

```python
import functools

import jax
import jax.numpy as jnp
from jax import lax
from jax.experimental import pallas as pl
from jax.experimental.pallas import tpu as pltpu
from jax.sharding import PartitionSpec as P

FRICTION = 0.1
TIME_STEP = 0.4
EDGE = 3
PAD = 8
VMEM_BYTES = 48 * 1024 * 1024
CHUNKS = 1


def parent_list(offspring):
    count = offspring.shape[0]
    running = jnp.cumsum(offspring)
    slots = jnp.arange(count, dtype=jnp.int32)
    return jnp.sum((running[None, :] <= slots[:, None]).astype(jnp.int32), axis=1)


def swap_edges(head, tail):
    count = lax.axis_size("tile")
    me = lax.axis_index("tile")
    above = jnp.zeros_like(head)
    below = jnp.zeros_like(head)
    for parity in range(2):
        pairs = []
        for i in range(parity, count - 1, 2):
            pairs += [(i, i + 1), (i + 1, i)]
        if pairs:
            upper = me % 2 == parity
            got = lax.ppermute(jnp.where(upper, tail, head), "tile", pairs)
            below = jnp.where(upper, got, below)
            above = jnp.where(upper, above, got)
    return above, below


def wind_window(wind, start_hour, row_count):
    count = lax.axis_size("tile")
    devices = lax.axis_size("dom")
    me = lax.axis_index("tile")
    hours_dev, parts, coarse_rows, coarse_cols = wind.shape
    own_rows = row_count // 2
    window = min(own_rows + PAD, coarse_rows)
    shared = devices % 2 == 0
    odd = lax.axis_index("dom") % 2

    def first_row(tile):
        return jnp.clip(tile * own_rows - PAD // 2, 0, coarse_rows - window)

    def panel(hour, tile):
        cells = lax.dynamic_slice(
            wind, (hour % hours_dev, 0, first_row(tile), 0), (1, parts, window, coarse_cols)
        )
        return cells.reshape(parts * window, coarse_cols)

    def fetch(hour):
        found = panel(hour, me)
        for shift in range(1, count):
            got = lax.ppermute(
                panel(hour, (me + shift) % count),
                "tile",
                [(i, (i + shift) % count) for i in range(count)],
            )
            found = jnp.where(hour // hours_dev == (me - shift) % count, got, found)
        return found

    if not shared:
        return jnp.concatenate([fetch(start_hour[0]), fetch(start_hour[0] + 1)]), first_row(me)
    found = fetch(start_hour[0] + odd)
    other = lax.ppermute(found, "dom", [(i, i ^ 1) for i in range(devices)])
    both = [jnp.where(odd == 0, found, other), jnp.where(odd == 0, other, found)]
    return jnp.concatenate(both), first_row(me)


def wind_kernel(where_ref, coarse_ref, fine_ref):
    hours, parts, rows, fine_cols = fine_ref.shape
    coarse_cols = fine_cols // 2
    window = coarse_ref.shape[0] // (hours * parts)
    first = where_ref[0]
    base = where_ref[1]
    fine_row = lax.broadcasted_iota(jnp.int32, (rows, window), 0) + first
    coarse_row = lax.broadcasted_iota(jnp.int32, (rows, window), 1) + base
    lift = jnp.where((fine_row >> 1) == coarse_row, 1.0, 0.0).astype(jnp.bfloat16)
    step = 128
    fine_col = lax.broadcasted_iota(jnp.int32, (step, 2 * step), 1)
    coarse_col = lax.broadcasted_iota(jnp.int32, (step, 2 * step), 0)
    widen = jnp.where((fine_col >> 1) == coarse_col, 1.0, 0.0).astype(jnp.bfloat16)
    for left in range(0, coarse_cols, step):
        cells = coarse_ref[:, left : left + step]
        wide_cells = jnp.dot(cells, widen, preferred_element_type=jnp.float32)
        for hour in range(hours):
            for part in range(parts):
                low = (hour * parts + part) * window
                panel = wide_cells[low : low + window].astype(jnp.bfloat16)
                tall = jnp.dot(lift, panel, preferred_element_type=jnp.float32)
                fine_ref[hour, part, :, 2 * left : 2 * (left + step)] = TIME_STEP * tall


def fine_wind(coarse, first, base, rows):
    hours, parts = 2, 2
    window, cols = coarse.shape[0] // (hours * parts), coarse.shape[1]
    return pl.pallas_call(
        wind_kernel,
        out_shape=jax.ShapeDtypeStruct((hours, parts, rows, 2 * cols), jnp.float32),
        in_specs=[
            pl.BlockSpec(memory_space=pltpu.SMEM),
            pl.BlockSpec(memory_space=pltpu.VMEM),
        ],
        out_specs=pl.BlockSpec(memory_space=pltpu.VMEM),
        compiler_params=pltpu.CompilerParams(vmem_limit_bytes=VMEM_BYTES),
        cost_estimate=pl.CostEstimate(
            flops=4 * hours * parts * rows * window * cols,
            bytes_accessed=8 * hours * parts * rows * cols,
            transcendentals=0,
        ),
    )(jnp.stack([first, base]).astype(jnp.int32), coarse)


def step_kernel(total_rows, where_ref, state_ref, depth_ref, wind_ref, out_ref, one, two, flux):
    rows = state_ref.shape[1]
    cols = state_ref.shape[2]
    blocks = rows // PAD
    first = where_ref[0]

    def shifted(ref, index, row, by):
        if 0 <= row + by <= rows - PAD:
            return ref[index, row + by : row + by + PAD, :]
        return pltpu.roll(ref[index, row : row + PAD, :], -by % PAD, 0)

    def across(field):
        return pltpu.roll(field, cols - 1, 1) - pltpu.roll(field, 1, 1)

    def section(source, stress, share, store, chosen):
        for block in range(blocks):
            low = block * PAD
            here = pl.ds(low, PAD)
            flux[0, here, :] = depth_ref[here, :] * source[2, here, :]
        for block in chosen:
            low = block * PAD
            here = pl.ds(low, PAD)
            row = first + low + lax.broadcasted_iota(jnp.int32, (PAD, 1), 0)
            turn = TIME_STEP * (0.1 + 0.4 * row.astype(jnp.float32) / total_rows)
            surface = source[0, here, :]
            east = source[1, here, :]
            north = source[2, here, :]
            flux_up = shifted(flux, 0, low, 1) - shifted(flux, 0, low, -1)
            next_surface = surface - (across(depth_ref[here, :] * east) + flux_up)
            rise = shifted(source, 0, low, 1) - shifted(source, 0, low, -1)
            half = 0.5 * TIME_STEP
            keep = 1.0 - TIME_STEP * FRICTION
            next_east = keep * east + turn * north - half * across(surface) + stress(0, here)
            next_north = keep * north - turn * east - half * rise + stress(1, here)
            inside = None
            if block == 0 or block == blocks - 1:
                inside = (row >= 0) & (row < total_rows)
            for part, value in enumerate((next_surface, next_east, next_north)):
                if share != 1.0:
                    value = (1.0 - share) * state_ref[part, here, :] + share * value
                if inside is not None:
                    value = jnp.where(inside, value, 0.0)
                store(part, low, value)

    def into(target):
        def store(part, low, value):
            target[part, pl.ds(low, PAD), :] = value

        return store

    def finish(part, low, value):
        out_ref[part, pl.ds(low - PAD, PAD), :] = value

    everything = range(blocks)
    section(state_ref, lambda part, here: wind_ref[0, part, here, :], 1.0, into(one), everything)
    section(one, lambda part, here: wind_ref[1, part, here, :], 0.25, into(two), everything)
    section(
        two,
        lambda part, here: 0.5 * (wind_ref[0, part, here, :] + wind_ref[1, part, here, :]),
        2.0 / 3.0,
        finish,
        range(1, blocks - 1),
    )


def step(state, depth, wind, first, total_rows):
    parts, rows, cols = state.shape
    own = rows - 2 * PAD
    vmem = pl.BlockSpec(memory_space=pltpu.VMEM)
    return pl.pallas_call(
        functools.partial(step_kernel, total_rows),
        out_shape=jax.ShapeDtypeStruct((parts, own, cols), jnp.float32),
        in_specs=[pl.BlockSpec(memory_space=pltpu.SMEM), vmem, vmem, vmem],
        out_specs=vmem,
        scratch_shapes=[
            pltpu.VMEM((parts, rows, cols), jnp.float32),
            pltpu.VMEM((parts, rows, cols), jnp.float32),
            pltpu.VMEM((1, rows, cols), jnp.float32),
        ],
        compiler_params=pltpu.CompilerParams(vmem_limit_bytes=VMEM_BYTES),
        cost_estimate=pl.CostEstimate(
            flops=100 * parts * rows * cols,
            bytes_accessed=4 * (3 * parts + 3) * rows * cols,
            transcendentals=0,
        ),
    )(first[None].astype(jnp.int32), state, depth, wind)


def exchange_all(cells, parents):
    spread = lax.all_to_all(cells[None], "dom", split_axis=3, concat_axis=0, tiled=True)
    picked = jnp.take(spread, parents, axis=0)
    return lax.all_to_all(picked, "dom", split_axis=0, concat_axis=3, tiled=True)[0]


def wide(array):
    return array.astype(jnp.float32)


def unit_of(pool, unit):
    return jnp.where(unit == 0, wide(pool[0])[None], wide(pool[1])[None])


class Near:
    def __init__(self):
        self.count = lax.axis_size("dom")
        self.groups = self.count // 4
        me = lax.axis_index("dom")
        self.group, self.pair, self.core = me // 4, me // 2 % 2, me % 2
        self.first = self.core == 0
        self.even_group = self.group ^ 1
        self.odd_group = ((self.group + 1) ^ 1) - 1

    def move(self, array, pairs):
        return lax.ppermute(array, "dom", pairs) if pairs else array

    def neighbour(self):
        return [(i, i ^ 1) for i in range(self.count)]

    def across(self, which):
        return [(i, i ^ 2) for i in range(self.count) if i % 2 == which]

    def along(self, which, parity):
        lower = [
            i
            for i in range(self.count - 4)
            if i % 2 == which and i // 4 % 2 == parity
        ]
        return [(i, i + 4) for i in lower] + [(i + 4, i) for i in lower]

    def halves(self, state):
        half = state.shape[1] // 2
        keep = lax.dynamic_slice_in_dim(state, self.core * half, half, 1)
        send = lax.dynamic_slice_in_dim(state, (1 - self.core) * half, half, 1)
        return keep, send.astype(jnp.float16)

    def pair_halves(self, keep, got):
        own = jnp.arange(2).reshape(2, 1, 1, 1) == self.core
        return jnp.where(own, keep[None], wide(got)[None]).astype(jnp.float16)

    def first_round(self, mine):
        one = self.move(mine, self.across(0) + self.along(1, 0))
        two = self.move(mine, self.along(1, 1))
        return mine, one, two

    def held(self, pools, parent):
        mine, one, two = lax.optimization_barrier(pools)
        unit = parent % 2
        place = parent // 4
        in_one = jnp.where(self.first, parent // 2 % 2 != self.pair, place == self.even_group)
        in_two = ~self.first & (place == self.odd_group) & ~in_one
        rest = jnp.where(in_one, unit_of(one, unit), unit_of(mine, unit))
        return jnp.where(in_two, unit_of(two, unit), rest)

    def wanted(self, parents, to_group, to_pair):
        base = 4 * jnp.clip(to_group, 0, self.groups - 1) + 2 * to_pair
        return lax.dynamic_slice_in_dim(parents, base, 2).reshape(2, 1, 1, 1)

    def second_round(self, pools, parents):
        first, pair = self.first, self.pair
        to_even = self.wanted(
            parents,
            jnp.where(first, self.even_group, self.group),
            jnp.where(first, pair, 1 - pair),
        )
        to_odd = self.wanted(parents, self.odd_group, pair)
        send = self.held(pools, to_even).astype(jnp.float16)
        three = self.move(send, self.along(0, 0) + self.across(1))
        send = self.held(pools, to_odd).astype(jnp.float16)
        four = self.move(send, self.along(0, 1))
        return three, four

    def slots(self, pools, three, four, parents):
        first = self.first
        parent = self.wanted(parents, self.group, self.pair)
        place = parent // 4
        in_three = jnp.where(first, place == self.even_group, parent // 2 % 2 != self.pair)
        in_four = first & (place == self.odd_group) & (place != self.group) & ~in_three
        both = jnp.where(in_three, wide(three), self.held(pools, parent))
        both = jnp.where(in_four, wide(four), both)
        own = jnp.where(first, both[0], both[1]).astype(jnp.float16)
        return own, jnp.where(first, both[1], both[0]).astype(jnp.float16)


def body(states, offspring, sea_depth, wind, start_hour):
    row_count = states.shape[2]
    total_rows = row_count * lax.axis_size("tile")
    first = lax.axis_index("tile") * row_count - PAD
    rows = row_count + 2 * PAD
    fill = ((PAD - EDGE, 0), (0, 0)), ((0, PAD - EDGE), (0, 0))
    parents = parent_list(offspring)
    slots = jnp.arange(parents.shape[0], dtype=jnp.int32)
    state = states[0]

    def surroundings(sea_depth, wind):
        coarse, base = wind_window(wind, start_hour, row_count)
        above, below = swap_edges(sea_depth[:EDGE], sea_depth[-EDGE:])
        return coarse, base, above, below

    def fields(sea_depth, coarse, base, above, below):
        depth = (0.5 * TIME_STEP) * jnp.concatenate(
            [jnp.pad(above, fill[0]), sea_depth, jnp.pad(below, fill[1])]
        )
        return depth, fine_wind(coarse, first, base, rows)

    def finish(parts, depth, stress):
        above, below = swap_edges(parts[0][:, :EDGE], parts[-1][:, -EDGE:])
        pieces = [jnp.pad(wide(above), ((0, 0),) + fill[0])]
        pieces += [wide(part) for part in parts]
        pieces += [jnp.pad(wide(below), ((0, 0),) + fill[1])]
        return step(jnp.concatenate(pieces, axis=1), depth, stress, first, total_rows)

    def far():
        around = surroundings(sea_depth, wind)
        copied = exchange_all(state.astype(jnp.float16), parents)
        return finish([copied], *fields(sea_depth, *around))

    def near():
        plan = Near()
        keep, send = plan.halves(state)
        got = plan.move(send, plan.neighbour())
        size = keep.shape[1] // CHUNKS
        pools = [
            plan.first_round(plan.pair_halves(keep[:, at : at + size], got[:, at : at + size]))
            for at in range(0, CHUNKS * size, size)
        ]
        mine, later_depth, later_wind = lax.optimization_barrier(
            ([pool[0] for pool in pools], sea_depth, wind)
        )
        pools = [(own,) + pool[1:] for own, pool in zip(mine, pools)]
        around = surroundings(later_depth, later_wind)
        pools[-1], around = lax.optimization_barrier((pools[-1], around))
        moved = [plan.second_round(pool, parents) for pool in pools]
        depth, stress = fields(sea_depth, *around)
        moved[-1], depth, stress = lax.optimization_barrier((moved[-1], depth, stress))
        upper, lower = [], []
        for pool, (three, four) in zip(pools, moved):
            own, other = plan.slots(pool, three, four, parents)
            other = plan.move(other, plan.neighbour())
            upper.append(jnp.where(plan.first, wide(own), wide(other)).astype(jnp.float16))
            lower.append(jnp.where(plan.first, wide(other), wide(own)).astype(jnp.float16))
        return finish(upper + lower, depth, stress)

    if parents.shape[0] % 4 or row_count % (2 * CHUNKS):
        return far()[None]
    close = jnp.all(jnp.abs(parents // 4 - slots // 4) <= 1)
    return lax.cond(close, near, far)[None]


def solution(mesh):
    return jax.shard_map(
        body,
        mesh=mesh,
        in_specs=(
            P("dom", None, "tile", None),
            P(),
            P("tile", None),
            P("tile", None, None, None),
            P(),
        ),
        out_specs=P("dom", None, "tile", None),
        check_vma=False,
    )
```

```python
import functools

import jax
import jax.numpy as jnp
from jax import lax
from jax.experimental import pallas as pl
from jax.experimental.pallas import tpu as pltpu
from jax.sharding import PartitionSpec as P

FRICTION = 0.1
TIME_STEP = 0.4
EDGE = 3
PAD = 8
WIND_VMEM = 10 * 1024 * 1024
STEP_VMEM = 20 * 1024 * 1024
CHUNKS = 2


def parents_by_starts(offspring):
    running = jnp.cumsum(offspring)
    return lambda slots: jnp.sum((running[None, :] <= slots[:, None]).astype(jnp.int32), axis=1)


def parents_by_ends(offspring):
    count = offspring.shape[0]
    index = jnp.arange(count)
    running = jnp.sum(jnp.where(index[None, :] <= index[:, None], offspring[None, :], 0), axis=1)
    return lambda slots: count - jnp.sum(
        (running[None, :] > slots[:, None]).astype(jnp.int32), axis=1
    )


def swap_edges(head, tail):
    count = lax.axis_size("tile")
    me = lax.axis_index("tile")
    above = jnp.zeros_like(head)
    below = jnp.zeros_like(head)
    for parity in range(2):
        pairs = []
        for i in range(parity, count - 1, 2):
            pairs += [(i, i + 1), (i + 1, i)]
        if pairs:
            upper = me % 2 == parity
            got = lax.ppermute(jnp.where(upper, tail, head), "tile", pairs)
            below = jnp.where(upper, got, below)
            above = jnp.where(upper, above, got)
    return above, below


def wind_window(wind, start_hour, row_count):
    count = lax.axis_size("tile")
    devices = lax.axis_size("dom")
    me = lax.axis_index("tile")
    hours_dev, parts, coarse_rows, coarse_cols = wind.shape
    own_rows = row_count // 2
    window = min(own_rows + PAD, coarse_rows)
    shared = devices % 2 == 0
    odd = lax.axis_index("dom") % 2

    def first_row(tile):
        return jnp.clip(tile * own_rows - PAD // 2, 0, coarse_rows - window)

    def panel(hour, tile):
        cells = lax.dynamic_slice(
            wind, (hour % hours_dev, 0, first_row(tile), 0), (1, parts, window, coarse_cols)
        )
        return cells.reshape(parts * window, coarse_cols)

    def fetch(hour):
        found = panel(hour, me)
        for shift in range(1, count):
            got = lax.ppermute(
                panel(hour, (me + shift) % count),
                "tile",
                [(i, (i + shift) % count) for i in range(count)],
            )
            found = jnp.where(hour // hours_dev == (me - shift) % count, got, found)
        return found

    if not shared:
        return [fetch(start_hour[0]), fetch(start_hour[0] + 1)], first_row(me)
    return [fetch(start_hour[0] + odd)], first_row(me)


def both_hours(panels):
    if len(panels) == 2:
        return jnp.concatenate(panels)
    odd = lax.axis_index("dom") % 2
    found = panels[0]
    other = lax.ppermute(found, "dom", [(i, i ^ 1) for i in range(lax.axis_size("dom"))])
    return jnp.concatenate(
        [jnp.where(odd == 0, found, other), jnp.where(odd == 0, other, found)]
    )


def wind_kernel(where_ref, coarse_ref, fine_ref):
    hours, parts, rows, fine_cols = fine_ref.shape
    coarse_cols = fine_cols // 2
    window = coarse_ref.shape[0] // (hours * parts)
    first = where_ref[0]
    base = where_ref[1]
    fine_row = lax.broadcasted_iota(jnp.int32, (rows, window), 0) + first
    coarse_row = lax.broadcasted_iota(jnp.int32, (rows, window), 1) + base
    lift = jnp.where((fine_row >> 1) == coarse_row, 1.0, 0.0).astype(jnp.bfloat16)
    step = 128
    fine_col = lax.broadcasted_iota(jnp.int32, (step, 2 * step), 1)
    coarse_col = lax.broadcasted_iota(jnp.int32, (step, 2 * step), 0)
    widen = jnp.where((fine_col >> 1) == coarse_col, 1.0, 0.0).astype(jnp.bfloat16)
    for left in range(0, coarse_cols, step):
        cells = coarse_ref[:, left : left + step]
        wide_cells = jnp.dot(cells, widen, preferred_element_type=jnp.float32)
        for hour in range(hours):
            for part in range(parts):
                low = (hour * parts + part) * window
                panel = wide_cells[low : low + window].astype(jnp.bfloat16)
                tall = jnp.dot(lift, panel, preferred_element_type=jnp.float32)
                fine_ref[hour, part, :, 2 * left : 2 * (left + step)] = TIME_STEP * tall


def fine_wind(coarse, first, base, rows):
    hours, parts = 2, 2
    window, cols = coarse.shape[0] // (hours * parts), coarse.shape[1]
    return pl.pallas_call(
        wind_kernel,
        out_shape=jax.ShapeDtypeStruct((hours, parts, rows, 2 * cols), jnp.float32),
        in_specs=[
            pl.BlockSpec(memory_space=pltpu.SMEM),
            pl.BlockSpec(memory_space=pltpu.VMEM),
        ],
        out_specs=pl.BlockSpec(memory_space=pltpu.VMEM),
        compiler_params=pltpu.CompilerParams(vmem_limit_bytes=WIND_VMEM),
        cost_estimate=pl.CostEstimate(
            flops=4 * hours * parts * rows * window * cols,
            bytes_accessed=8 * hours * parts * rows * cols,
            transcendentals=0,
        ),
    )(jnp.stack([first, base]).astype(jnp.int32), coarse)


def step_kernel(total_rows, where_ref, state_ref, depth_ref, wind_ref, out_ref, one, two, flux):
    rows = state_ref.shape[1]
    cols = state_ref.shape[2]
    blocks = rows // PAD
    first = where_ref[0]

    def shifted(ref, index, row, by):
        if 0 <= row + by <= rows - PAD:
            return ref[index, row + by : row + by + PAD, :]
        return pltpu.roll(ref[index, row : row + PAD, :], -by % PAD, 0)

    def across(field):
        return pltpu.roll(field, cols - 1, 1) - pltpu.roll(field, 1, 1)

    def section(source, stress, share, store, chosen):
        for block in range(blocks):
            low = block * PAD
            here = pl.ds(low, PAD)
            flux[0, here, :] = depth_ref[here, :] * source[2, here, :]
        for block in chosen:
            low = block * PAD
            here = pl.ds(low, PAD)
            row = first + low + lax.broadcasted_iota(jnp.int32, (PAD, 1), 0)
            turn = TIME_STEP * (0.1 + 0.4 * row.astype(jnp.float32) / total_rows)
            surface = source[0, here, :]
            east = source[1, here, :]
            north = source[2, here, :]
            flux_up = shifted(flux, 0, low, 1) - shifted(flux, 0, low, -1)
            next_surface = surface - (across(depth_ref[here, :] * east) + flux_up)
            rise = shifted(source, 0, low, 1) - shifted(source, 0, low, -1)
            half = 0.5 * TIME_STEP
            keep = 1.0 - TIME_STEP * FRICTION
            next_east = keep * east + turn * north - half * across(surface) + stress(0, here)
            next_north = keep * north - turn * east - half * rise + stress(1, here)
            inside = None
            if block == 0 or block == blocks - 1:
                inside = (row >= 0) & (row < total_rows)
            for part, value in enumerate((next_surface, next_east, next_north)):
                if share != 1.0:
                    value = (1.0 - share) * state_ref[part, here, :] + share * value
                if inside is not None:
                    value = jnp.where(inside, value, 0.0)
                store(part, low, value)

    def into(target):
        def store(part, low, value):
            target[part, pl.ds(low, PAD), :] = value

        return store

    def finish(part, low, value):
        out_ref[part, pl.ds(low - PAD, PAD), :] = value

    everything = range(blocks)
    section(state_ref, lambda part, here: wind_ref[0, part, here, :], 1.0, into(one), everything)
    section(one, lambda part, here: wind_ref[1, part, here, :], 0.25, into(two), everything)
    section(
        two,
        lambda part, here: 0.5 * (wind_ref[0, part, here, :] + wind_ref[1, part, here, :]),
        2.0 / 3.0,
        finish,
        range(1, blocks - 1),
    )


def step(state, depth, wind, first, total_rows):
    parts, rows, cols = state.shape
    own = rows - 2 * PAD
    vmem = pl.BlockSpec(memory_space=pltpu.VMEM)
    return pl.pallas_call(
        functools.partial(step_kernel, total_rows),
        out_shape=jax.ShapeDtypeStruct((parts, own, cols), jnp.float32),
        in_specs=[pl.BlockSpec(memory_space=pltpu.SMEM), vmem, vmem, vmem],
        out_specs=vmem,
        scratch_shapes=[
            pltpu.VMEM((parts, rows, cols), jnp.float32),
            pltpu.VMEM((parts, rows, cols), jnp.float32),
            pltpu.VMEM((1, rows, cols), jnp.float32),
        ],
        compiler_params=pltpu.CompilerParams(vmem_limit_bytes=STEP_VMEM),
        cost_estimate=pl.CostEstimate(
            flops=100 * parts * rows * cols,
            bytes_accessed=4 * (3 * parts + 3) * rows * cols,
            transcendentals=0,
        ),
    )(first[None].astype(jnp.int32), state, depth, wind)


def exchange_all(cells, parents):
    spread = lax.all_to_all(cells[None], "dom", split_axis=3, concat_axis=0, tiled=True)
    picked = jnp.take(spread, parents, axis=0)
    return lax.all_to_all(picked, "dom", split_axis=0, concat_axis=3, tiled=True)[0]


def wide(array):
    return array.astype(jnp.float32)


def picked(pools, code):
    units = [pool[unit] for pool in pools for unit in range(2)]
    result = wide(units[0])[None]
    for at, unit in enumerate(units[1:], 1):
        result = jnp.where(code == at, wide(unit)[None], result)
    return result


def once(cells, array):
    row = wide(cells[0, 0, :1, : array.shape[-1]])
    return jnp.where(jnp.abs(row) > 1e30, jnp.zeros_like(array), array)


class Near:
    def __init__(self):
        self.count = lax.axis_size("dom")
        self.groups = self.count // 4
        me = lax.axis_index("dom")
        self.group, self.pair, self.core = me // 4, me // 2 % 2, me % 2
        self.first = self.core == 0
        self.even_group = self.group ^ 1
        self.odd_group = ((self.group + 1) ^ 1) - 1

    def move(self, array, pairs):
        return lax.ppermute(array, "dom", pairs) if pairs else array

    def neighbour(self):
        return [(i, i ^ 1) for i in range(self.count)]

    def across(self, which):
        return [(i, i ^ 2) for i in range(self.count) if i % 2 == which]

    def along(self, which, parity):
        lower = [
            i
            for i in range(self.count - 4)
            if i % 2 == which and i // 4 % 2 == parity
        ]
        return [(i, i + 4) for i in lower] + [(i + 4, i) for i in lower]

    def halves(self, state):
        half = state.shape[1] // 2
        keep = lax.dynamic_slice_in_dim(state, self.core * half, half, 1)
        send = lax.dynamic_slice_in_dim(state, (1 - self.core) * half, half, 1)
        return keep, send.astype(jnp.float16)

    def pair_halves(self, keep, got):
        own = jnp.arange(2).reshape(2, 1, 1, 1) == self.core
        return jnp.where(own, keep[None], wide(got)[None]).astype(jnp.float16)

    def first_round(self, mine):
        one = self.move(mine, self.across(0) + self.along(1, 0))
        two = self.move(mine, self.along(1, 1))
        return mine, one, two

    def held(self, parent):
        place = parent // 4
        in_one = jnp.where(self.first, parent // 2 % 2 != self.pair, place == self.even_group)
        in_two = ~self.first & (place == self.odd_group) & ~in_one
        return parent % 2 + jnp.where(in_two, 4, jnp.where(in_one, 2, 0))

    def codes(self, parents_of):
        first, pair, group = self.first, self.pair, self.group
        entry = jnp.arange(6)
        kind, unit = entry // 2, entry % 2
        unit = jnp.where(kind == 2, unit ^ self.core, unit)
        to_group = jnp.where(kind == 0, jnp.where(first, self.even_group, group), group)
        to_group = jnp.where(kind == 1, self.odd_group, to_group)
        to_pair = jnp.where((kind == 0) & ~first, 1 - pair, pair)
        parent = parents_of(4 * jnp.clip(to_group, 0, self.groups - 1) + 2 * to_pair + unit)
        place = parent // 4
        in_three = jnp.where(first, place == self.even_group, parent // 2 % 2 != pair)
        in_four = first & (place == self.odd_group) & (place != group) & ~in_three
        here = jnp.where(in_three, 6 + unit, jnp.where(in_four, 8 + unit, self.held(parent)))
        code = jnp.where(kind == 2, here, self.held(parent)).reshape(-1, 1, 1, 1)
        return code[:2], code[2:4], code[4:]

    def to_send(self, pools, codes):
        return [picked(pools, code) for code in codes[:2]]

    def second_round(self, even, odd):
        three = self.move(even, self.along(0, 0) + self.across(1))
        return three, self.move(odd, self.along(0, 1))

    def slots(self, pools, codes):
        both = picked(pools, codes[2]).astype(jnp.float16)
        return both[0], both[1]


def body(states, offspring, sea_depth, wind, start_hour):
    row_count = states.shape[2]
    total_rows = row_count * lax.axis_size("tile")
    first = lax.axis_index("tile") * row_count - PAD
    rows = row_count + 2 * PAD
    fill = ((PAD - EDGE, 0), (0, 0)), ((0, PAD - EDGE), (0, 0))
    slots = jnp.arange(offspring.shape[0], dtype=jnp.int32)
    parents = parents_by_starts(offspring)(slots)
    state = states[0]

    def surroundings(sea_depth, wind):
        panels, base = wind_window(wind, start_hour, row_count)
        return panels, base, *swap_edges(sea_depth[:EDGE], sea_depth[-EDGE:])

    def fields(sea_depth, coarse, base, above, below):
        depth = (0.5 * TIME_STEP) * jnp.concatenate(
            [jnp.pad(above, fill[0]), sea_depth, jnp.pad(below, fill[1])]
        )
        return depth, fine_wind(coarse, first, base, rows)

    def finish(parts, depth, stress):
        above, below = swap_edges(parts[0][:, :EDGE], parts[-1][:, -EDGE:])
        pieces = [jnp.pad(wide(above), ((0, 0),) + fill[0])]
        pieces += [wide(part) for part in parts]
        pieces += [jnp.pad(wide(below), ((0, 0),) + fill[1])]
        return step(jnp.concatenate(pieces, axis=1), depth, stress, first, total_rows)

    def far():
        panels, *edges = surroundings(sea_depth, wind)
        copied = exchange_all(state.astype(jnp.float16), parents)
        return finish([copied], *fields(sea_depth, both_hours(panels), *edges))

    def near():
        plan = Near()
        after = lax.optimization_barrier
        keep, send = after(plan.halves(state))
        got = plan.move(send, plan.neighbour())
        size = keep.shape[1] // CHUNKS
        pools = [
            plan.first_round(plan.pair_halves(keep[:, at : at + size], got[:, at : at + size]))
            for at in range(0, CHUNKS * size, size)
        ]
        mine, near_depth, near_wind, near_offspring = after(
            ([pool[0] for pool in pools], sea_depth, wind, offspring)
        )
        pools = [(own,) + pool[1:] for own, pool in zip(mine, pools)]
        panels, *edges = surroundings(near_depth, near_wind)
        moved, ready = [None] * CHUNKS, None
        codes = [plan.codes(ways(near_offspring)) for ways in (parents_by_starts, parents_by_ends)]
        for at in reversed(range(CHUNKS)):
            sends = plan.to_send(pools[at], codes[at % 2])
            if ready:
                sends = [once(cells, send) for cells, send in zip(ready, sends)]
            ready = [send.astype(jnp.float16) for send in sends]
            moved[at] = plan.second_round(*ready)
        panels = [once(ready[1], panel) for panel in panels]
        edges[1:] = [once(ready[1], edge) for edge in edges[1:]]
        coarse = both_hours(panels)
        depth, stress = fields(near_depth, coarse, *edges)
        moved[0], depth, stress = after((moved[0], depth, stress))
        upper, lower = [], []
        for at in range(CHUNKS):
            own, other = plan.slots(pools[at] + moved[at], codes[at % 2])
            got = plan.move(other, plan.neighbour())
            upper.append(jnp.where(plan.first, wide(own), wide(got)).astype(jnp.float16))
            lower.append(jnp.where(plan.first, wide(got), wide(own)).astype(jnp.float16))
        return finish(upper + lower, depth, stress)

    if parents.shape[0] % 4 or row_count % (2 * CHUNKS):
        return far()[None]
    close = jnp.all(jnp.abs(parents // 4 - slots // 4) <= 1)
    return lax.cond(close, near, far)[None]


def solution(mesh):
    return jax.shard_map(
        body,
        mesh=mesh,
        in_specs=(
            P("dom", None, "tile", None),
            P(),
            P("tile", None),
            P("tile", None, None, None),
            P(),
        ),
        out_specs=P("dom", None, "tile", None),
        check_vma=False,
    )
```

```python
import functools

import jax
import jax.numpy as jnp
from jax import lax
from jax.experimental import pallas as pl
from jax.experimental.pallas import tpu as pltpu
from jax.sharding import PartitionSpec as P

FRICTION = 0.1
TIME_STEP = 0.4
EDGE = 3
PAD = 8
WIND_VMEM = 10 * 1024 * 1024
STEP_VMEM = 20 * 1024 * 1024
CHUNKS = 2


def parents_by_starts(offspring):
    running = jnp.cumsum(offspring)
    return lambda slots: jnp.sum((running[None, :] <= slots[:, None]).astype(jnp.int32), axis=1)


def parents_by_ends(offspring):
    count = offspring.shape[0]
    index = jnp.arange(count)
    running = jnp.sum(jnp.where(index[None, :] <= index[:, None], offspring[None, :], 0), axis=1)
    return lambda slots: count - jnp.sum(
        (running[None, :] > slots[:, None]).astype(jnp.int32), axis=1
    )


def swap_edges(head, tail):
    count = lax.axis_size("tile")
    me = lax.axis_index("tile")
    above = jnp.zeros_like(head)
    below = jnp.zeros_like(head)
    for parity in range(2):
        pairs = []
        for i in range(parity, count - 1, 2):
            pairs += [(i, i + 1), (i + 1, i)]
        if pairs:
            upper = me % 2 == parity
            got = lax.ppermute(jnp.where(upper, tail, head), "tile", pairs)
            below = jnp.where(upper, got, below)
            above = jnp.where(upper, above, got)
    return above, below


def wind_window(wind, start_hour, row_count):
    count = lax.axis_size("tile")
    devices = lax.axis_size("dom")
    me = lax.axis_index("tile")
    hours_dev, parts, coarse_rows, coarse_cols = wind.shape
    own_rows = row_count // 2
    window = min(own_rows + PAD, coarse_rows)
    shared = devices % 2 == 0
    odd = lax.axis_index("dom") % 2

    def first_row(tile):
        return jnp.clip(tile * own_rows - PAD // 2, 0, coarse_rows - window)

    def panel(hour, tile):
        cells = lax.dynamic_slice(
            wind, (hour % hours_dev, 0, first_row(tile), 0), (1, parts, window, coarse_cols)
        )
        return cells.reshape(parts * window, coarse_cols)

    def fetch(hour):
        found = panel(hour, me)
        for shift in range(1, count):
            got = lax.ppermute(
                panel(hour, (me + shift) % count),
                "tile",
                [(i, (i + shift) % count) for i in range(count)],
            )
            found = jnp.where(hour // hours_dev == (me - shift) % count, got, found)
        return found

    if not shared:
        return [fetch(start_hour[0]), fetch(start_hour[0] + 1)], first_row(me)
    return [fetch(start_hour[0] + odd)], first_row(me)


def both_hours(panels):
    if len(panels) == 2:
        return jnp.concatenate(panels)
    odd = lax.axis_index("dom") % 2
    found = panels[0]
    other = lax.ppermute(found, "dom", [(i, i ^ 1) for i in range(lax.axis_size("dom"))])
    return jnp.concatenate(
        [jnp.where(odd == 0, found, other), jnp.where(odd == 0, other, found)]
    )


def wind_kernel(where_ref, coarse_ref, fine_ref):
    hours, parts, rows, fine_cols = fine_ref.shape
    coarse_cols = fine_cols // 2
    window = coarse_ref.shape[0] // (hours * parts)
    first = where_ref[0]
    base = where_ref[1]
    fine_row = lax.broadcasted_iota(jnp.int32, (rows, window), 0) + first
    coarse_row = lax.broadcasted_iota(jnp.int32, (rows, window), 1) + base
    lift = jnp.where((fine_row >> 1) == coarse_row, 1.0, 0.0).astype(jnp.bfloat16)
    step = 128
    fine_col = lax.broadcasted_iota(jnp.int32, (step, 2 * step), 1)
    coarse_col = lax.broadcasted_iota(jnp.int32, (step, 2 * step), 0)
    widen = jnp.where((fine_col >> 1) == coarse_col, 1.0, 0.0).astype(jnp.bfloat16)
    for left in range(0, coarse_cols, step):
        cells = coarse_ref[:, left : left + step]
        wide_cells = jnp.dot(cells, widen, preferred_element_type=jnp.float32)
        for hour in range(hours):
            for part in range(parts):
                low = (hour * parts + part) * window
                panel = wide_cells[low : low + window].astype(jnp.bfloat16)
                tall = jnp.dot(lift, panel, preferred_element_type=jnp.float32)
                fine_ref[hour, part, :, 2 * left : 2 * (left + step)] = TIME_STEP * tall


def fine_wind(coarse, first, base, rows):
    hours, parts = 2, 2
    window, cols = coarse.shape[0] // (hours * parts), coarse.shape[1]
    return pl.pallas_call(
        wind_kernel,
        out_shape=jax.ShapeDtypeStruct((hours, parts, rows, 2 * cols), jnp.float32),
        in_specs=[
            pl.BlockSpec(memory_space=pltpu.SMEM),
            pl.BlockSpec(memory_space=pltpu.VMEM),
        ],
        out_specs=pl.BlockSpec(memory_space=pltpu.VMEM),
        compiler_params=pltpu.CompilerParams(vmem_limit_bytes=WIND_VMEM),
        cost_estimate=pl.CostEstimate(
            flops=4 * hours * parts * rows * window * cols,
            bytes_accessed=8 * hours * parts * rows * cols,
            transcendentals=0,
        ),
    )(jnp.stack([first, base]).astype(jnp.int32), coarse)


def sections(state_ref, depth_ref, wind_at, one, two, flux, base, first, total_rows, store, closed):
    rows = state_ref.shape[1]
    cols = state_ref.shape[2]
    blocks = rows // PAD

    def shifted(ref, index, row, by):
        if 0 <= row + by <= rows - PAD:
            return ref[index, row + by : row + by + PAD, :]
        turned = pltpu.roll(ref[index, row : row + PAD, :], -by % PAD, 0)
        if not closed:
            return turned
        at = lax.broadcasted_iota(jnp.int32, (PAD, 1), 0)
        return jnp.where(at == (0 if by < 0 else PAD - 1), 0.0, turned)

    def across(field):
        return pltpu.roll(field, cols - 1, 1) - pltpu.roll(field, 1, 1)

    def section(source, stress, share, put):
        for block in range(blocks):
            here = pl.ds(block * PAD, PAD)
            there = pl.ds(base + block * PAD, PAD)
            flux[0, here, :] = depth_ref[there, :] * source[2, here, :]
        for block in range(blocks):
            low = block * PAD
            here = pl.ds(low, PAD)
            there = pl.ds(base + low, PAD)
            row = first + low + lax.broadcasted_iota(jnp.int32, (PAD, 1), 0)
            turn = TIME_STEP * (0.1 + 0.4 * row.astype(jnp.float32) / total_rows)
            surface = source[0, here, :]
            east = source[1, here, :]
            north = source[2, here, :]
            flux_up = shifted(flux, 0, low, 1) - shifted(flux, 0, low, -1)
            next_surface = surface - (across(depth_ref[there, :] * east) + flux_up)
            rise = shifted(source, 0, low, 1) - shifted(source, 0, low, -1)
            half = 0.5 * TIME_STEP
            keep = 1.0 - TIME_STEP * FRICTION
            next_east = keep * east + turn * north - half * across(surface) + stress(0, there)
            next_north = keep * north - turn * east - half * rise + stress(1, there)
            values = [next_surface, next_east, next_north]
            if share != 1.0:
                values = [
                    (1.0 - share) * state_ref[part, here, :] + share * value
                    for part, value in enumerate(values)
                ]
            put(block, values)

    def into(target):
        def put(block, values):
            for part, value in enumerate(values):
                target[part, pl.ds(block * PAD, PAD), :] = value

        return put

    section(state_ref, lambda part, there: wind_at[0, part, there, :], 1.0, into(one))
    section(one, lambda part, there: wind_at[1, part, there, :], 0.25, into(two))
    section(
        two,
        lambda part, there: 0.5 * (wind_at[0, part, there, :] + wind_at[1, part, there, :]),
        2.0 / 3.0,
        store,
    )


def step_kernel(total_rows, where_ref, state_ref, depth_ref, wind_ref, out_ref, one, two, flux, done, sems):
    rows = state_ref.shape[1]

    def write(block):
        here = pl.ds(block * PAD, PAD)
        return pltpu.make_async_copy(done.at[:, here], out_ref.at[:, here], sems.at[block])

    def store(block, values):
        for part, value in enumerate(values):
            done[part, pl.ds(block * PAD, PAD), :] = value
        write(block).start()

    first = where_ref[0] + PAD
    sections(
        state_ref, depth_ref, wind_ref, one, two, flux, PAD, first, total_rows, store, True
    )
    for block in range(rows // PAD):
        write(block).wait()


def step(state, depth, wind, first, total_rows):
    parts, rows, cols = state.shape
    vmem = pl.BlockSpec(memory_space=pltpu.VMEM)
    return pl.pallas_call(
        functools.partial(step_kernel, total_rows),
        out_shape=jax.ShapeDtypeStruct((parts, rows, cols), jnp.float32),
        in_specs=[pl.BlockSpec(memory_space=pltpu.SMEM), vmem, vmem, vmem],
        out_specs=pl.BlockSpec(memory_space=pltpu.HBM),
        scratch_shapes=[
            pltpu.VMEM((parts, rows, cols), jnp.float32),
            pltpu.VMEM((parts, rows, cols), jnp.float32),
            pltpu.VMEM((1, rows, cols), jnp.float32),
            pltpu.VMEM((parts, rows, cols), jnp.float32),
            pltpu.SemaphoreType.DMA((rows // PAD,)),
        ],
        compiler_params=pltpu.CompilerParams(vmem_limit_bytes=STEP_VMEM),
        cost_estimate=pl.CostEstimate(
            flops=100 * parts * rows * cols,
            bytes_accessed=4 * (3 * parts + 3) * rows * cols,
            transcendentals=0,
        ),
    )(first[None].astype(jnp.int32), state, depth, wind)


def edge_kernel(
    total_rows, where_ref, above_ref, below_ref, depth_ref, wind_ref, old_ref, out_ref,
    one, two, flux, done, kept, sems,
):
    rows = out_ref.shape[1]
    first = where_ref[0]

    def edge(window, base, block, at, used):
        here = pl.ds(at, PAD)
        read = pltpu.make_async_copy(old_ref.at[:, here], kept, sems.at[0])
        write = pltpu.make_async_copy(done, out_ref.at[:, here], sems.at[1])
        read.start()

        def store(number, values):
            if number != block:
                return
            read.wait()
            row = lax.broadcasted_iota(jnp.int32, (PAD, 1), 0)
            for part, value in enumerate(values):
                done[part] = jnp.where(used(row), value, kept[part])
            write.start()

        sections(
            window, depth_ref, wind_ref, one, two, flux, base, first + base, total_rows, store, False
        )
        write.wait()

    @pl.when(first + PAD > 0)
    def _():
        edge(above_ref, 0, 1, 0, lambda row: row < EDGE)

    @pl.when(first + PAD + rows < total_rows)
    def _():
        edge(below_ref, rows, 0, rows - PAD, lambda row: row >= PAD - EDGE)


def mend(result, above, below, depth, wind, first, total_rows):
    parts, rows, cols = result.shape
    vmem = pl.BlockSpec(memory_space=pltpu.VMEM)
    hbm = pl.BlockSpec(memory_space=pltpu.HBM)
    window = pltpu.VMEM((parts, 2 * PAD, cols), jnp.float32)
    return pl.pallas_call(
        functools.partial(edge_kernel, total_rows),
        out_shape=jax.ShapeDtypeStruct((parts, rows, cols), jnp.float32),
        in_specs=[pl.BlockSpec(memory_space=pltpu.SMEM), vmem, vmem, vmem, vmem, hbm],
        out_specs=hbm,
        scratch_shapes=[
            window,
            window,
            pltpu.VMEM((1, 2 * PAD, cols), jnp.float32),
            pltpu.VMEM((parts, PAD, cols), jnp.float32),
            pltpu.VMEM((parts, PAD, cols), jnp.float32),
            pltpu.SemaphoreType.DMA((2,)),
        ],
        input_output_aliases={5: 0},
        compiler_params=pltpu.CompilerParams(vmem_limit_bytes=STEP_VMEM),
        cost_estimate=pl.CostEstimate(
            flops=200 * parts * PAD * cols,
            bytes_accessed=100 * parts * PAD * cols,
            transcendentals=0,
        ),
    )(first[None].astype(jnp.int32), above, below, depth, wind, result)


def exchange_all(cells, parents):
    spread = lax.all_to_all(cells[None], "dom", split_axis=3, concat_axis=0, tiled=True)
    picked = jnp.take(spread, parents, axis=0)
    return lax.all_to_all(picked, "dom", split_axis=0, concat_axis=3, tiled=True)[0]


def wide(array):
    return array.astype(jnp.float32)


def picked(pools, code):
    units = [pool[unit] for pool in pools for unit in range(2)]
    result = wide(units[0])[None]
    for at, unit in enumerate(units[1:], 1):
        result = jnp.where(code == at, wide(unit)[None], result)
    return result


def once(cells, array):
    row = wide(cells[0, 0, :1, : array.shape[-1]])
    return jnp.where(jnp.abs(row) > 1e30, jnp.zeros_like(array), array)


class Near:
    def __init__(self):
        self.count = lax.axis_size("dom")
        self.groups = self.count // 4
        me = lax.axis_index("dom")
        self.group, self.pair, self.core = me // 4, me // 2 % 2, me % 2
        self.first = self.core == 0
        self.even_group = self.group ^ 1
        self.odd_group = ((self.group + 1) ^ 1) - 1

    def move(self, array, pairs):
        return lax.ppermute(array, "dom", pairs) if pairs else array

    def neighbour(self):
        return [(i, i ^ 1) for i in range(self.count)]

    def across(self, which):
        return [(i, i ^ 2) for i in range(self.count) if i % 2 == which]

    def along(self, which, parity):
        lower = [
            i
            for i in range(self.count - 4)
            if i % 2 == which and i // 4 % 2 == parity
        ]
        return [(i, i + 4) for i in lower] + [(i + 4, i) for i in lower]

    def halves(self, state):
        half = state.shape[1] // 2
        keep = lax.dynamic_slice_in_dim(state, self.core * half, half, 1)
        send = lax.dynamic_slice_in_dim(state, (1 - self.core) * half, half, 1)
        return keep, send.astype(jnp.float16)

    def pair_halves(self, keep, got):
        own = jnp.arange(2).reshape(2, 1, 1, 1) == self.core
        return jnp.where(own, keep[None], wide(got)[None]).astype(jnp.float16)

    def first_round(self, mine):
        one = self.move(mine, self.across(0) + self.along(1, 0))
        two = self.move(mine, self.along(1, 1))
        return mine, one, two

    def held(self, parent):
        place = parent // 4
        in_one = jnp.where(self.first, parent // 2 % 2 != self.pair, place == self.even_group)
        in_two = ~self.first & (place == self.odd_group) & ~in_one
        return parent % 2 + jnp.where(in_two, 4, jnp.where(in_one, 2, 0))

    def codes(self, parents_of):
        first, pair, group = self.first, self.pair, self.group
        entry = jnp.arange(6)
        kind, unit = entry // 2, entry % 2
        unit = jnp.where(kind == 2, unit ^ self.core, unit)
        to_group = jnp.where(kind == 0, jnp.where(first, self.even_group, group), group)
        to_group = jnp.where(kind == 1, self.odd_group, to_group)
        to_pair = jnp.where((kind == 0) & ~first, 1 - pair, pair)
        parent = parents_of(4 * jnp.clip(to_group, 0, self.groups - 1) + 2 * to_pair + unit)
        place = parent // 4
        in_three = jnp.where(first, place == self.even_group, parent // 2 % 2 != pair)
        in_four = first & (place == self.odd_group) & (place != group) & ~in_three
        here = jnp.where(in_three, 6 + unit, jnp.where(in_four, 8 + unit, self.held(parent)))
        code = jnp.where(kind == 2, here, self.held(parent)).reshape(-1, 1, 1, 1)
        return code[:2], code[2:4], code[4:]

    def to_send(self, pools, codes):
        return [picked(pools, code) for code in codes[:2]]

    def second_round(self, even, odd):
        three = self.move(even, self.along(0, 0) + self.across(1))
        return three, self.move(odd, self.along(0, 1))

    def slots(self, pools, codes):
        both = picked(pools, codes[2]).astype(jnp.float16)
        return both[0], both[1]


def body(states, offspring, sea_depth, wind, start_hour):
    row_count = states.shape[2]
    total_rows = row_count * lax.axis_size("tile")
    first = lax.axis_index("tile") * row_count - PAD
    rows = row_count + 2 * PAD
    fill = ((PAD - EDGE, 0), (0, 0)), ((0, PAD - EDGE), (0, 0))
    slots = jnp.arange(offspring.shape[0], dtype=jnp.int32)
    parents = parents_by_starts(offspring)(slots)
    state = states[0]

    def surroundings(sea_depth, wind):
        panels, base = wind_window(wind, start_hour, row_count)
        return panels, base, *swap_edges(sea_depth[:EDGE], sea_depth[-EDGE:])

    def fields(sea_depth, coarse, base, above, below):
        depth = (0.5 * TIME_STEP) * jnp.concatenate(
            [jnp.pad(above, fill[0]), sea_depth, jnp.pad(below, fill[1])]
        )
        return depth, fine_wind(coarse, first, base, rows)

    def finish(parts, depth, stress):
        above, below = swap_edges(parts[0][:, :EDGE], parts[-1][:, -EDGE:])
        result = step(
            jnp.concatenate([wide(part) for part in parts], axis=1), depth, stress, first, total_rows
        )
        above = [jnp.pad(wide(above), ((0, 0),) + fill[0]), wide(parts[0][:, :PAD])]
        below = [wide(parts[-1][:, -PAD:]), jnp.pad(wide(below), ((0, 0),) + fill[1])]
        above, below = [jnp.concatenate(window, axis=1) for window in (above, below)]
        return mend(result, above, below, depth, stress, first, total_rows)

    def far():
        panels, *edges = surroundings(sea_depth, wind)
        copied = exchange_all(state.astype(jnp.float16), parents)
        return finish([copied], *fields(sea_depth, both_hours(panels), *edges))

    def near():
        plan = Near()
        after = lax.optimization_barrier
        keep, send = after(plan.halves(state))
        got = plan.move(send, plan.neighbour())
        size = keep.shape[1] // CHUNKS
        pools = [
            plan.first_round(plan.pair_halves(keep[:, at : at + size], got[:, at : at + size]))
            for at in range(0, CHUNKS * size, size)
        ]
        mine, near_depth, near_wind, near_offspring = after(
            ([pool[0] for pool in pools], sea_depth, wind, offspring)
        )
        pools = [(own,) + pool[1:] for own, pool in zip(mine, pools)]
        panels, *edges = surroundings(near_depth, near_wind)
        moved, ready = [None] * CHUNKS, None
        codes = [plan.codes(ways(near_offspring)) for ways in (parents_by_starts, parents_by_ends)]
        for at in reversed(range(CHUNKS)):
            sends = plan.to_send(pools[at], codes[at % 2])
            if ready:
                sends = [once(cells, send) for cells, send in zip(ready, sends)]
            ready = [send.astype(jnp.float16) for send in sends]
            moved[at] = plan.second_round(*ready)
        panels = [once(ready[1], panel) for panel in panels]
        edges[1:] = [once(ready[1], edge) for edge in edges[1:]]
        coarse = both_hours(panels)
        depth, stress = fields(near_depth, coarse, *edges)
        moved[0], depth, stress = after((moved[0], depth, stress))
        upper, lower = [], []
        for at in range(CHUNKS):
            own, other = plan.slots(pools[at] + moved[at], codes[at % 2])
            got = plan.move(other, plan.neighbour())
            upper.append(jnp.where(plan.first, wide(own), wide(got)).astype(jnp.float16))
            lower.append(jnp.where(plan.first, wide(got), wide(own)).astype(jnp.float16))
        return finish(upper + lower, depth, stress)

    if parents.shape[0] % 4 or row_count % (2 * CHUNKS):
        return far()[None]
    close = jnp.all(jnp.abs(parents // 4 - slots // 4) <= 1)
    return lax.cond(close, near, far)[None]


def solution(mesh):
    return jax.shard_map(
        body,
        mesh=mesh,
        in_specs=(
            P("dom", None, "tile", None),
            P(),
            P("tile", None),
            P("tile", None, None, None),
            P(),
        ),
        out_specs=P("dom", None, "tile", None),
        check_vma=False,
    )
```

```python
import functools

import jax
import jax.numpy as jnp
from jax import lax
from jax.experimental import pallas as pl
from jax.experimental.pallas import tpu as pltpu
from jax.sharding import PartitionSpec as P

FRICTION = 0.1
TIME_STEP = 0.4
EDGE = 3
PAD = 8
WIND_VMEM = 10 * 1024 * 1024
STEP_VMEM = 20 * 1024 * 1024
CHUNKS = 2


def parents_by_starts(offspring):
    running = jnp.cumsum(offspring)
    return lambda slots: jnp.sum((running[None, :] <= slots[:, None]).astype(jnp.int32), axis=1)


def parents_by_ends(offspring):
    count = offspring.shape[0]
    index = jnp.arange(count)
    running = jnp.sum(jnp.where(index[None, :] <= index[:, None], offspring[None, :], 0), axis=1)
    return lambda slots: count - jnp.sum(
        (running[None, :] > slots[:, None]).astype(jnp.int32), axis=1
    )


def swap_edges(head, tail):
    count = lax.axis_size("tile")
    me = lax.axis_index("tile")
    above = jnp.zeros_like(head)
    below = jnp.zeros_like(head)
    for parity in range(2):
        pairs = []
        for i in range(parity, count - 1, 2):
            pairs += [(i, i + 1), (i + 1, i)]
        if pairs:
            upper = me % 2 == parity
            got = lax.ppermute(jnp.where(upper, tail, head), "tile", pairs)
            below = jnp.where(upper, got, below)
            above = jnp.where(upper, above, got)
    return above, below


def tall_edge(edge, cols):
    pieces = jnp.concatenate([edge[:, at : at + cols] for at in range(0, edge.shape[1], cols)])
    high = lax.reduce_precision(pieces, 8, 7)
    return [high.astype(jnp.bfloat16), (pieces - high).astype(jnp.bfloat16)]


def wide_edge(tall, rows, pieces):
    size = rows * pieces
    both = wide(tall[:size]) + wide(tall[size : 2 * size])
    return jnp.concatenate([both[at : at + rows] for at in range(0, size, rows)], axis=1)


def surroundings(sea_depth, wind, start_hour):
    count = lax.axis_size("tile")
    devices = lax.axis_size("dom")
    me = lax.axis_index("tile")
    hours_dev, parts, coarse_rows, coarse_cols = wind.shape
    row_count = sea_depth.shape[0]
    own_rows = row_count // 2
    window = min(own_rows + PAD, coarse_rows)
    odd = lax.axis_index("dom") % 2
    hours = [start_hour[0] + odd] if devices % 2 == 0 else [start_hour[0], start_hour[0] + 1]

    def first_row(tile):
        return jnp.clip(tile * own_rows - PAD // 2, 0, coarse_rows - window)

    def panels(tile):
        return [
            lax.dynamic_slice(
                wind, (hour % hours_dev, 0, first_row(tile), 0), (1, parts, window, coarse_cols)
            ).reshape(parts * window, coarse_cols)
            for hour in hours
        ]

    sent = []
    for shift in range(1, count):
        target = (me + shift) % count
        edge = jnp.where(target > me, sea_depth[-EDGE:], sea_depth[:EDGE])
        message = jnp.concatenate(panels(target) + tall_edge(edge, coarse_cols))
        pairs = [(i, (i + shift) % count) for i in range(count)]
        sent.append(lax.ppermute(message, "tile", pairs))
    return jnp.concatenate(panels(me)), sent, hours, first_row(me)


def assembled(sea_depth, wind, around):
    found, sent, hours, _ = around
    count = lax.axis_size("tile")
    devices = lax.axis_size("dom")
    me = lax.axis_index("tile")
    hours_dev = wind.shape[0]
    size = found.shape[0]
    part = size // len(hours)
    pieces = sea_depth.shape[1] // found.shape[1]
    above = jnp.zeros_like(sea_depth[:EDGE])
    below = jnp.zeros_like(sea_depth[:EDGE])
    owner = jnp.concatenate([jnp.full((part, 1), 0) + hour // hours_dev for hour in hours])
    for shift, message in enumerate(sent, 1):
        source = (me - shift) % count
        found = jnp.where(owner == source, message[:size], found)
        edge = wide_edge(message[size:], EDGE, pieces)
        above = jnp.where(source == me - 1, edge, above)
        below = jnp.where(source == me + 1, edge, below)
    if len(hours) == 2:
        return found, above, below
    odd = lax.axis_index("dom") % 2
    other = lax.ppermute(found, "dom", [(i, i ^ 1) for i in range(devices)])
    both = [jnp.where(odd == 0, found, other), jnp.where(odd == 0, other, found)]
    return jnp.concatenate(both), above, below


def wind_kernel(where_ref, coarse_ref, fine_ref):
    hours, parts, rows, fine_cols = fine_ref.shape
    coarse_cols = fine_cols // 2
    window = coarse_ref.shape[0] // (hours * parts)
    first = where_ref[0]
    base = where_ref[1]
    fine_row = lax.broadcasted_iota(jnp.int32, (rows, window), 0) + first
    coarse_row = lax.broadcasted_iota(jnp.int32, (rows, window), 1) + base
    lift = jnp.where((fine_row >> 1) == coarse_row, 1.0, 0.0).astype(jnp.bfloat16)
    step = 128
    fine_col = lax.broadcasted_iota(jnp.int32, (step, 2 * step), 1)
    coarse_col = lax.broadcasted_iota(jnp.int32, (step, 2 * step), 0)
    widen = jnp.where((fine_col >> 1) == coarse_col, 1.0, 0.0).astype(jnp.bfloat16)
    for left in range(0, coarse_cols, step):
        cells = coarse_ref[:, left : left + step]
        wide_cells = jnp.dot(cells, widen, preferred_element_type=jnp.float32)
        for hour in range(hours):
            for part in range(parts):
                low = (hour * parts + part) * window
                panel = wide_cells[low : low + window].astype(jnp.bfloat16)
                tall = jnp.dot(lift, panel, preferred_element_type=jnp.float32)
                fine_ref[hour, part, :, 2 * left : 2 * (left + step)] = TIME_STEP * tall


def fine_wind(coarse, first, base, rows):
    hours, parts = 2, 2
    window, cols = coarse.shape[0] // (hours * parts), coarse.shape[1]
    return pl.pallas_call(
        wind_kernel,
        out_shape=jax.ShapeDtypeStruct((hours, parts, rows, 2 * cols), jnp.float32),
        in_specs=[
            pl.BlockSpec(memory_space=pltpu.SMEM),
            pl.BlockSpec(memory_space=pltpu.VMEM),
        ],
        out_specs=pl.BlockSpec(memory_space=pltpu.VMEM),
        compiler_params=pltpu.CompilerParams(vmem_limit_bytes=WIND_VMEM),
        cost_estimate=pl.CostEstimate(
            flops=4 * hours * parts * rows * window * cols,
            bytes_accessed=8 * hours * parts * rows * cols,
            transcendentals=0,
        ),
    )(jnp.stack([first, base]).astype(jnp.int32), coarse)


def sections(state_ref, depth_ref, wind_at, one, two, flux, base, first, total_rows, store, closed):
    rows = state_ref.shape[1]
    cols = state_ref.shape[2]
    blocks = rows // PAD

    def shifted(ref, index, row, by):
        if 0 <= row + by <= rows - PAD:
            return ref[index, row + by : row + by + PAD, :]
        turned = pltpu.roll(ref[index, row : row + PAD, :], -by % PAD, 0)
        if not closed:
            return turned
        at = lax.broadcasted_iota(jnp.int32, (PAD, 1), 0)
        return jnp.where(at == (0 if by < 0 else PAD - 1), 0.0, turned)

    def across(field):
        return pltpu.roll(field, cols - 1, 1) - pltpu.roll(field, 1, 1)

    def section(source, stress, share, put):
        for block in range(blocks):
            here = pl.ds(block * PAD, PAD)
            there = pl.ds(base + block * PAD, PAD)
            flux[0, here, :] = depth_ref[there, :] * source[2, here, :]
        for block in range(blocks):
            low = block * PAD
            here = pl.ds(low, PAD)
            there = pl.ds(base + low, PAD)
            row = first + low + lax.broadcasted_iota(jnp.int32, (PAD, 1), 0)
            turn = TIME_STEP * (0.1 + 0.4 * row.astype(jnp.float32) / total_rows)
            surface = source[0, here, :]
            east = source[1, here, :]
            north = source[2, here, :]
            flux_up = shifted(flux, 0, low, 1) - shifted(flux, 0, low, -1)
            next_surface = surface - (across(depth_ref[there, :] * east) + flux_up)
            rise = shifted(source, 0, low, 1) - shifted(source, 0, low, -1)
            half = 0.5 * TIME_STEP
            keep = 1.0 - TIME_STEP * FRICTION
            next_east = keep * east + turn * north - half * across(surface) + stress(0, there)
            next_north = keep * north - turn * east - half * rise + stress(1, there)
            values = [next_surface, next_east, next_north]
            if share != 1.0:
                values = [
                    (1.0 - share) * state_ref[part, here, :] + share * value
                    for part, value in enumerate(values)
                ]
            put(block, values)

    def into(target):
        def put(block, values):
            for part, value in enumerate(values):
                target[part, pl.ds(block * PAD, PAD), :] = value

        return put

    section(state_ref, lambda part, there: wind_at[0, part, there, :], 1.0, into(one))
    section(one, lambda part, there: wind_at[1, part, there, :], 0.25, into(two))
    section(
        two,
        lambda part, there: 0.5 * (wind_at[0, part, there, :] + wind_at[1, part, there, :]),
        2.0 / 3.0,
        store,
    )


def step_kernel(total_rows, where_ref, state_ref, depth_ref, wind_ref, out_ref, one, two, flux, done, sems):
    rows = state_ref.shape[1]

    def write(block):
        here = pl.ds(block * PAD, PAD)
        return pltpu.make_async_copy(done.at[:, here], out_ref.at[:, here], sems.at[block])

    def store(block, values):
        for part, value in enumerate(values):
            done[part, pl.ds(block * PAD, PAD), :] = value
        write(block).start()

    first = where_ref[0] + PAD
    sections(
        state_ref, depth_ref, wind_ref, one, two, flux, PAD, first, total_rows, store, True
    )
    for block in range(rows // PAD):
        write(block).wait()


def step(state, depth, wind, first, total_rows):
    parts, rows, cols = state.shape
    vmem = pl.BlockSpec(memory_space=pltpu.VMEM)
    return pl.pallas_call(
        functools.partial(step_kernel, total_rows),
        out_shape=jax.ShapeDtypeStruct((parts, rows, cols), jnp.float32),
        in_specs=[pl.BlockSpec(memory_space=pltpu.SMEM), vmem, vmem, vmem],
        out_specs=pl.BlockSpec(memory_space=pltpu.HBM),
        scratch_shapes=[
            pltpu.VMEM((parts, rows, cols), jnp.float32),
            pltpu.VMEM((parts, rows, cols), jnp.float32),
            pltpu.VMEM((1, rows, cols), jnp.float32),
            pltpu.VMEM((parts, rows, cols), jnp.float32),
            pltpu.SemaphoreType.DMA((rows // PAD,)),
        ],
        compiler_params=pltpu.CompilerParams(vmem_limit_bytes=STEP_VMEM),
        cost_estimate=pl.CostEstimate(
            flops=100 * parts * rows * cols,
            bytes_accessed=4 * (3 * parts + 3) * rows * cols,
            transcendentals=0,
        ),
    )(first[None].astype(jnp.int32), state, depth, wind)


def edge_kernel(
    total_rows, where_ref, above_ref, below_ref, depth_ref, wind_ref, old_ref, out_ref,
    one, two, flux, done, kept, sems,
):
    rows = out_ref.shape[1]
    first = where_ref[0]

    def edge(window, base, block, at, used):
        here = pl.ds(at, PAD)
        read = pltpu.make_async_copy(old_ref.at[:, here], kept, sems.at[0])
        write = pltpu.make_async_copy(done, out_ref.at[:, here], sems.at[1])
        read.start()

        def store(number, values):
            if number != block:
                return
            read.wait()
            row = lax.broadcasted_iota(jnp.int32, (PAD, 1), 0)
            for part, value in enumerate(values):
                done[part] = jnp.where(used(row), value, kept[part])
            write.start()

        sections(
            window, depth_ref, wind_ref, one, two, flux, base, first + base, total_rows, store, False
        )
        write.wait()

    @pl.when(first + PAD > 0)
    def _():
        edge(above_ref, 0, 1, 0, lambda row: row < EDGE)

    @pl.when(first + PAD + rows < total_rows)
    def _():
        edge(below_ref, rows, 0, rows - PAD, lambda row: row >= PAD - EDGE)


def mend(result, above, below, depth, wind, first, total_rows):
    parts, rows, cols = result.shape
    vmem = pl.BlockSpec(memory_space=pltpu.VMEM)
    hbm = pl.BlockSpec(memory_space=pltpu.HBM)
    window = pltpu.VMEM((parts, 2 * PAD, cols), jnp.float32)
    return pl.pallas_call(
        functools.partial(edge_kernel, total_rows),
        out_shape=jax.ShapeDtypeStruct((parts, rows, cols), jnp.float32),
        in_specs=[pl.BlockSpec(memory_space=pltpu.SMEM), vmem, vmem, vmem, vmem, hbm],
        out_specs=hbm,
        scratch_shapes=[
            window,
            window,
            pltpu.VMEM((1, 2 * PAD, cols), jnp.float32),
            pltpu.VMEM((parts, PAD, cols), jnp.float32),
            pltpu.VMEM((parts, PAD, cols), jnp.float32),
            pltpu.SemaphoreType.DMA((2,)),
        ],
        input_output_aliases={5: 0},
        compiler_params=pltpu.CompilerParams(vmem_limit_bytes=STEP_VMEM),
        cost_estimate=pl.CostEstimate(
            flops=200 * parts * PAD * cols,
            bytes_accessed=100 * parts * PAD * cols,
            transcendentals=0,
        ),
    )(first[None].astype(jnp.int32), above, below, depth, wind, result)


def exchange_all(cells, parents):
    spread = lax.all_to_all(cells[None], "dom", split_axis=3, concat_axis=0, tiled=True)
    picked = jnp.take(spread, parents, axis=0)
    return lax.all_to_all(picked, "dom", split_axis=0, concat_axis=3, tiled=True)[0]


def wide(array):
    return array.astype(jnp.float32)


def picked(pools, code):
    units = [pool[unit] for pool in pools for unit in range(2)]
    result = wide(units[0])[None]
    for at, unit in enumerate(units[1:], 1):
        result = jnp.where(code == at, wide(unit)[None], result)
    return result


def once(cells, array):
    row = wide(cells[0, 0, :1, : array.shape[-1]])
    return jnp.where(jnp.abs(row) > 1e30, jnp.zeros_like(array), array)


class Near:
    def __init__(self):
        self.count = lax.axis_size("dom")
        self.groups = self.count // 4
        me = lax.axis_index("dom")
        self.group, self.pair, self.core = me // 4, me // 2 % 2, me % 2
        self.first = self.core == 0
        self.even_group = self.group ^ 1
        self.odd_group = ((self.group + 1) ^ 1) - 1

    def move(self, array, pairs):
        return lax.ppermute(array, "dom", pairs) if pairs else array

    def neighbour(self):
        return [(i, i ^ 1) for i in range(self.count)]

    def across(self, which):
        return [(i, i ^ 2) for i in range(self.count) if i % 2 == which]

    def along(self, which, parity):
        lower = [
            i
            for i in range(self.count - 4)
            if i % 2 == which and i // 4 % 2 == parity
        ]
        return [(i, i + 4) for i in lower] + [(i + 4, i) for i in lower]

    def halves(self, state):
        half = state.shape[1] // 2
        keep = lax.dynamic_slice_in_dim(state, self.core * half, half, 1)
        send = lax.dynamic_slice_in_dim(state, (1 - self.core) * half, half, 1)
        return keep, send.astype(jnp.float16)

    def pair_halves(self, keep, got):
        own = jnp.arange(2).reshape(2, 1, 1, 1) == self.core
        return jnp.where(own, keep[None], wide(got)[None]).astype(jnp.float16)

    def first_round(self, mine):
        one = self.move(mine, self.across(0) + self.along(1, 0))
        two = self.move(mine, self.along(1, 1))
        return mine, one, two

    def held(self, parent):
        place = parent // 4
        in_one = jnp.where(self.first, parent // 2 % 2 != self.pair, place == self.even_group)
        in_two = ~self.first & (place == self.odd_group) & ~in_one
        return parent % 2 + jnp.where(in_two, 4, jnp.where(in_one, 2, 0))

    def codes(self, parents_of):
        first, pair, group = self.first, self.pair, self.group
        entry = jnp.arange(6)
        kind, unit = entry // 2, entry % 2
        unit = jnp.where(kind == 2, unit ^ self.core, unit)
        to_group = jnp.where(kind == 0, jnp.where(first, self.even_group, group), group)
        to_group = jnp.where(kind == 1, self.odd_group, to_group)
        to_pair = jnp.where((kind == 0) & ~first, 1 - pair, pair)
        parent = parents_of(4 * jnp.clip(to_group, 0, self.groups - 1) + 2 * to_pair + unit)
        place = parent // 4
        in_three = jnp.where(first, place == self.even_group, parent // 2 % 2 != pair)
        in_four = first & (place == self.odd_group) & (place != group) & ~in_three
        here = jnp.where(in_three, 6 + unit, jnp.where(in_four, 8 + unit, self.held(parent)))
        code = jnp.where(kind == 2, here, self.held(parent)).reshape(-1, 1, 1, 1)
        return code[:2], code[2:4], code[4:]

    def to_send(self, pools, codes):
        return [picked(pools, code) for code in codes[:2]]

    def second_round(self, even, odd):
        three = self.move(even, self.along(0, 0) + self.across(1))
        return three, self.move(odd, self.along(0, 1))

    def slots(self, pools, codes):
        both = picked(pools, codes[2]).astype(jnp.float16)
        return both[0], both[1]


def body(states, offspring, sea_depth, wind, start_hour):
    row_count = states.shape[2]
    total_rows = row_count * lax.axis_size("tile")
    first = lax.axis_index("tile") * row_count - PAD
    rows = row_count + 2 * PAD
    fill = ((PAD - EDGE, 0), (0, 0)), ((0, PAD - EDGE), (0, 0))
    slots = jnp.arange(offspring.shape[0], dtype=jnp.int32)
    parents = parents_by_starts(offspring)(slots)
    state = states[0]

    def fields(around):
        coarse, above, below = assembled(sea_depth, wind, around)
        depth = (0.5 * TIME_STEP) * jnp.concatenate(
            [jnp.pad(above, fill[0]), sea_depth, jnp.pad(below, fill[1])]
        )
        return depth, fine_wind(coarse, first, around[-1], rows)

    def finish(parts, depth, stress):
        above, below = swap_edges(parts[0][:, :EDGE], parts[-1][:, -EDGE:])
        result = step(
            jnp.concatenate([wide(part) for part in parts], axis=1), depth, stress, first, total_rows
        )
        above = [jnp.pad(wide(above), ((0, 0),) + fill[0]), wide(parts[0][:, :PAD])]
        below = [wide(parts[-1][:, -PAD:]), jnp.pad(wide(below), ((0, 0),) + fill[1])]
        above, below = [jnp.concatenate(window, axis=1) for window in (above, below)]
        return mend(result, above, below, depth, stress, first, total_rows)

    def far():
        around = surroundings(sea_depth, wind, start_hour)
        copied = exchange_all(state.astype(jnp.float16), parents)
        return finish([copied], *fields(around))

    def near():
        plan = Near()
        after = lax.optimization_barrier
        keep, send = after(plan.halves(state))
        got = plan.move(send, plan.neighbour())
        size = keep.shape[1] // CHUNKS
        pools = [
            plan.first_round(plan.pair_halves(keep[:, at : at + size], got[:, at : at + size]))
            for at in range(0, CHUNKS * size, size)
        ]
        mine, near_depth, near_wind, near_offspring = after(
            ([pool[0] for pool in pools], sea_depth, wind, offspring)
        )
        pools = [(own,) + pool[1:] for own, pool in zip(mine, pools)]
        own, sent, *rest = surroundings(near_depth, near_wind, start_hour)
        moved, ready = [None] * CHUNKS, None
        codes = [plan.codes(ways(near_offspring)) for ways in (parents_by_starts, parents_by_ends)]
        for at in reversed(range(CHUNKS)):
            sends = plan.to_send(pools[at], codes[at % 2])
            if ready:
                sends = [once(cells, send) for cells, send in zip(ready, sends)]
            ready = [send.astype(jnp.float16) for send in sends]
            moved[at] = plan.second_round(*ready)
        depth, stress = fields((own, [once(ready[1], message) for message in sent], *rest))
        moved[0], depth, stress = after((moved[0], depth, stress))
        upper, lower = [], []
        for at in range(CHUNKS):
            own, other = plan.slots(pools[at] + moved[at], codes[at % 2])
            got = plan.move(other, plan.neighbour())
            upper.append(jnp.where(plan.first, wide(own), wide(got)).astype(jnp.float16))
            lower.append(jnp.where(plan.first, wide(got), wide(own)).astype(jnp.float16))
        return finish(upper + lower, depth, stress)

    if parents.shape[0] % 4 or row_count % (2 * CHUNKS):
        return far()[None]
    close = jnp.all(jnp.abs(parents // 4 - slots // 4) <= 1)
    return lax.cond(close, near, far)[None]


def solution(mesh):
    return jax.shard_map(
        body,
        mesh=mesh,
        in_specs=(
            P("dom", None, "tile", None),
            P(),
            P("tile", None),
            P("tile", None, None, None),
            P(),
        ),
        out_specs=P("dom", None, "tile", None),
        check_vma=False,
    )
```

```python
import functools

import jax
import jax.numpy as jnp
from jax import lax
from jax.experimental import pallas as pl
from jax.experimental.pallas import tpu as pltpu
from jax.sharding import PartitionSpec as P

FRICTION = 0.1
TIME_STEP = 0.4
EDGE = 3
PAD = 8
WIND_VMEM = 10 * 1024 * 1024
STEP_VMEM = 20 * 1024 * 1024
CHUNKS = 2


def parents_by_starts(offspring):
    running = jnp.cumsum(offspring)
    return lambda slots: jnp.sum((running[None, :] <= slots[:, None]).astype(jnp.int32), axis=1)


def parents_by_ends(offspring):
    count = offspring.shape[0]
    index = jnp.arange(count)
    running = jnp.sum(jnp.where(index[None, :] <= index[:, None], offspring[None, :], 0), axis=1)
    return lambda slots: count - jnp.sum(
        (running[None, :] > slots[:, None]).astype(jnp.int32), axis=1
    )


def swap_edges(head, tail):
    count = lax.axis_size("tile")
    me = lax.axis_index("tile")
    above = jnp.zeros_like(head)
    below = jnp.zeros_like(head)
    for parity in range(2):
        pairs = []
        for i in range(parity, count - 1, 2):
            pairs += [(i, i + 1), (i + 1, i)]
        if pairs:
            upper = me % 2 == parity
            got = lax.ppermute(jnp.where(upper, tail, head), "tile", pairs)
            below = jnp.where(upper, got, below)
            above = jnp.where(upper, above, got)
    return above, below


def tall_edge(edge, cols):
    pieces = jnp.concatenate([edge[:, at : at + cols] for at in range(0, edge.shape[1], cols)])
    high = lax.reduce_precision(pieces, 8, 7)
    return [high.astype(jnp.bfloat16), (pieces - high).astype(jnp.bfloat16)]


def wide_edge(tall, rows, pieces):
    size = rows * pieces
    both = wide(tall[:size]) + wide(tall[size : 2 * size])
    return jnp.concatenate([both[at : at + rows] for at in range(0, size, rows)], axis=1)


def surroundings(sea_depth, wind, start_hour):
    count = lax.axis_size("tile")
    devices = lax.axis_size("dom")
    me = lax.axis_index("tile")
    hours_dev, parts, coarse_rows, coarse_cols = wind.shape
    row_count = sea_depth.shape[0]
    own_rows = row_count // 2
    window = min(own_rows + PAD, coarse_rows)
    odd = lax.axis_index("dom") % 2
    hours = [start_hour[0] + odd] if devices % 2 == 0 else [start_hour[0], start_hour[0] + 1]

    def first_row(tile):
        return jnp.clip(tile * own_rows - PAD // 2, 0, coarse_rows - window)

    def panels(tile):
        return [
            lax.dynamic_slice(
                wind, (hour % hours_dev, 0, first_row(tile), 0), (1, parts, window, coarse_cols)
            ).reshape(parts * window, coarse_cols)
            for hour in hours
        ]

    sent = []
    for shift in range(1, count):
        target = (me + shift) % count
        edge = jnp.where(target > me, sea_depth[-EDGE:], sea_depth[:EDGE])
        message = jnp.concatenate(panels(target) + tall_edge(edge, coarse_cols))
        pairs = [(i, (i + shift) % count) for i in range(count)]
        sent.append(lax.ppermute(message, "tile", pairs))
    return jnp.concatenate(panels(me)), sent, hours, first_row(me)


def assembled(sea_depth, wind, around):
    found, sent, hours, _ = around
    count = lax.axis_size("tile")
    devices = lax.axis_size("dom")
    me = lax.axis_index("tile")
    hours_dev = wind.shape[0]
    size = found.shape[0]
    part = size // len(hours)
    pieces = sea_depth.shape[1] // found.shape[1]
    above = jnp.zeros_like(sea_depth[:EDGE])
    below = jnp.zeros_like(sea_depth[:EDGE])
    owner = jnp.concatenate([jnp.full((part, 1), 0) + hour // hours_dev for hour in hours])
    for shift, message in enumerate(sent, 1):
        source = (me - shift) % count
        found = jnp.where(owner == source, message[:size], found)
        edge = wide_edge(message[size:], EDGE, pieces)
        above = jnp.where(source == me - 1, edge, above)
        below = jnp.where(source == me + 1, edge, below)
    if len(hours) == 2:
        return found, above, below
    odd = lax.axis_index("dom") % 2
    other = lax.ppermute(found, "dom", [(i, i ^ 1) for i in range(devices)])
    both = [jnp.where(odd == 0, found, other), jnp.where(odd == 0, other, found)]
    return jnp.concatenate(both), above, below


def wind_kernel(where_ref, coarse_ref, fine_ref):
    hours, parts, rows, fine_cols = fine_ref.shape
    coarse_cols = fine_cols // 2
    window = coarse_ref.shape[0] // (hours * parts)
    first = where_ref[0]
    base = where_ref[1]
    fine_row = lax.broadcasted_iota(jnp.int32, (rows, window), 0) + first
    coarse_row = lax.broadcasted_iota(jnp.int32, (rows, window), 1) + base
    lift = jnp.where((fine_row >> 1) == coarse_row, 1.0, 0.0).astype(jnp.bfloat16)
    step = 128
    fine_col = lax.broadcasted_iota(jnp.int32, (step, 2 * step), 1)
    coarse_col = lax.broadcasted_iota(jnp.int32, (step, 2 * step), 0)
    widen = jnp.where((fine_col >> 1) == coarse_col, 1.0, 0.0).astype(jnp.bfloat16)
    for left in range(0, coarse_cols, step):
        cells = coarse_ref[:, left : left + step]
        wide_cells = jnp.dot(cells, widen, preferred_element_type=jnp.float32)
        for hour in range(hours):
            for part in range(parts):
                low = (hour * parts + part) * window
                panel = wide_cells[low : low + window].astype(jnp.bfloat16)
                tall = jnp.dot(lift, panel, preferred_element_type=jnp.float32)
                fine_ref[hour, part, :, 2 * left : 2 * (left + step)] = TIME_STEP * tall


def fine_wind(coarse, first, base, rows):
    hours, parts = 2, 2
    window, cols = coarse.shape[0] // (hours * parts), coarse.shape[1]
    return pl.pallas_call(
        wind_kernel,
        out_shape=jax.ShapeDtypeStruct((hours, parts, rows, 2 * cols), jnp.float32),
        in_specs=[
            pl.BlockSpec(memory_space=pltpu.SMEM),
            pl.BlockSpec(memory_space=pltpu.VMEM),
        ],
        out_specs=pl.BlockSpec(memory_space=pltpu.VMEM),
        compiler_params=pltpu.CompilerParams(vmem_limit_bytes=WIND_VMEM),
        cost_estimate=pl.CostEstimate(
            flops=4 * hours * parts * rows * window * cols,
            bytes_accessed=8 * hours * parts * rows * cols,
            transcendentals=0,
        ),
    )(jnp.stack([first, base]).astype(jnp.int32), coarse)


def sections(state_ref, depth_ref, wind_at, one, two, flux, base, first, total_rows, store, closed):
    rows = state_ref.shape[1]
    cols = state_ref.shape[2]
    blocks = rows // PAD

    def shifted(ref, index, row, by):
        if 0 <= row + by <= rows - PAD:
            return ref[index, row + by : row + by + PAD, :]
        turned = pltpu.roll(ref[index, row : row + PAD, :], -by % PAD, 0)
        if not closed:
            return turned
        at = lax.broadcasted_iota(jnp.int32, (PAD, 1), 0)
        return jnp.where(at == (0 if by < 0 else PAD - 1), 0.0, turned)

    def across(field):
        return pltpu.roll(field, cols - 1, 1) - pltpu.roll(field, 1, 1)

    def section(source, stress, share, put):
        for block in range(blocks):
            here = pl.ds(block * PAD, PAD)
            there = pl.ds(base + block * PAD, PAD)
            flux[0, here, :] = depth_ref[there, :] * source[2, here, :]
        for block in range(blocks):
            low = block * PAD
            here = pl.ds(low, PAD)
            there = pl.ds(base + low, PAD)
            row = first + low + lax.broadcasted_iota(jnp.int32, (PAD, 1), 0)
            turn = TIME_STEP * (0.1 + 0.4 * row.astype(jnp.float32) / total_rows)
            surface = source[0, here, :]
            east = source[1, here, :]
            north = source[2, here, :]
            flux_up = shifted(flux, 0, low, 1) - shifted(flux, 0, low, -1)
            next_surface = surface - (across(depth_ref[there, :] * east) + flux_up)
            rise = shifted(source, 0, low, 1) - shifted(source, 0, low, -1)
            half = 0.5 * TIME_STEP
            keep = 1.0 - TIME_STEP * FRICTION
            next_east = keep * east + turn * north - half * across(surface) + stress(0, there)
            next_north = keep * north - turn * east - half * rise + stress(1, there)
            values = [next_surface, next_east, next_north]
            if share != 1.0:
                values = [
                    (1.0 - share) * state_ref[part, here, :] + share * value
                    for part, value in enumerate(values)
                ]
            put(block, values)

    def into(target):
        def put(block, values):
            for part, value in enumerate(values):
                target[part, pl.ds(block * PAD, PAD), :] = value

        return put

    section(state_ref, lambda part, there: wind_at[0, part, there, :], 1.0, into(one))
    section(one, lambda part, there: wind_at[1, part, there, :], 0.25, into(two))
    section(
        two,
        lambda part, there: 0.5 * (wind_at[0, part, there, :] + wind_at[1, part, there, :]),
        2.0 / 3.0,
        store,
    )


def step_kernel(total_rows, where_ref, state_ref, depth_ref, wind_ref, out_ref, one, two, flux, done, sems):
    rows = state_ref.shape[1]

    def write(block):
        here = pl.ds(block * PAD, PAD)
        return pltpu.make_async_copy(done.at[:, here], out_ref.at[:, here], sems.at[block])

    def store(block, values):
        for part, value in enumerate(values):
            done[part, pl.ds(block * PAD, PAD), :] = value
        write(block).start()

    first = where_ref[0] + PAD
    sections(
        state_ref, depth_ref, wind_ref, one, two, flux, PAD, first, total_rows, store, True
    )
    for block in range(rows // PAD):
        write(block).wait()


def step(state, depth, wind, first, total_rows):
    parts, rows, cols = state.shape
    vmem = pl.BlockSpec(memory_space=pltpu.VMEM)
    return pl.pallas_call(
        functools.partial(step_kernel, total_rows),
        out_shape=jax.ShapeDtypeStruct((parts, rows, cols), jnp.float32),
        in_specs=[pl.BlockSpec(memory_space=pltpu.SMEM), vmem, vmem, vmem],
        out_specs=pl.BlockSpec(memory_space=pltpu.HBM),
        scratch_shapes=[
            pltpu.VMEM((parts, rows, cols), jnp.float32),
            pltpu.VMEM((parts, rows, cols), jnp.float32),
            pltpu.VMEM((1, rows, cols), jnp.float32),
            pltpu.VMEM((parts, rows, cols), jnp.float32),
            pltpu.SemaphoreType.DMA((rows // PAD,)),
        ],
        compiler_params=pltpu.CompilerParams(vmem_limit_bytes=STEP_VMEM),
        cost_estimate=pl.CostEstimate(
            flops=100 * parts * rows * cols,
            bytes_accessed=4 * (3 * parts + 3) * rows * cols,
            transcendentals=0,
        ),
    )(first[None].astype(jnp.int32), state, depth, wind)


def edge_kernel(
    total_rows, where_ref, above_ref, below_ref, depth_ref, wind_ref, old_ref, out_ref,
    one, two, flux, done, kept, sems,
):
    rows = out_ref.shape[1]
    first = where_ref[0]

    def edge(window, base, block, at, used):
        here = pl.ds(at, PAD)
        read = pltpu.make_async_copy(old_ref.at[:, here], kept, sems.at[0])
        write = pltpu.make_async_copy(done, out_ref.at[:, here], sems.at[1])
        read.start()

        def store(number, values):
            if number != block:
                return
            read.wait()
            row = lax.broadcasted_iota(jnp.int32, (PAD, 1), 0)
            for part, value in enumerate(values):
                done[part] = jnp.where(used(row), value, kept[part])
            write.start()

        sections(
            window, depth_ref, wind_ref, one, two, flux, base, first + base, total_rows, store, False
        )
        write.wait()

    @pl.when(first + PAD > 0)
    def _():
        edge(above_ref, 0, 1, 0, lambda row: row < EDGE)

    @pl.when(first + PAD + rows < total_rows)
    def _():
        edge(below_ref, rows, 0, rows - PAD, lambda row: row >= PAD - EDGE)


def mend(result, above, below, depth, wind, first, total_rows):
    parts, rows, cols = result.shape
    vmem = pl.BlockSpec(memory_space=pltpu.VMEM)
    hbm = pl.BlockSpec(memory_space=pltpu.HBM)
    window = pltpu.VMEM((parts, 2 * PAD, cols), jnp.float32)
    return pl.pallas_call(
        functools.partial(edge_kernel, total_rows),
        out_shape=jax.ShapeDtypeStruct((parts, rows, cols), jnp.float32),
        in_specs=[pl.BlockSpec(memory_space=pltpu.SMEM), vmem, vmem, vmem, vmem, hbm],
        out_specs=hbm,
        scratch_shapes=[
            window,
            window,
            pltpu.VMEM((1, 2 * PAD, cols), jnp.float32),
            pltpu.VMEM((parts, PAD, cols), jnp.float32),
            pltpu.VMEM((parts, PAD, cols), jnp.float32),
            pltpu.SemaphoreType.DMA((2,)),
        ],
        input_output_aliases={5: 0},
        compiler_params=pltpu.CompilerParams(vmem_limit_bytes=STEP_VMEM),
        cost_estimate=pl.CostEstimate(
            flops=200 * parts * PAD * cols,
            bytes_accessed=100 * parts * PAD * cols,
            transcendentals=0,
        ),
    )(first[None].astype(jnp.int32), above, below, depth, wind, result)


def exchange_all(cells, parents):
    spread = lax.all_to_all(cells[None], "dom", split_axis=3, concat_axis=0, tiled=True)
    picked = jnp.take(spread, parents, axis=0, mode="clip")
    return lax.all_to_all(picked, "dom", split_axis=0, concat_axis=3, tiled=True)[0]


def wide(array):
    return array.astype(jnp.float32)


def picked(pools, code):
    units = [pool[unit] for pool in pools for unit in range(2)]
    result = wide(units[0])[None]
    for at, unit in enumerate(units[1:], 1):
        result = jnp.where(code == at, wide(unit)[None], result)
    return result


def once(cells, array):
    row = wide(cells[0, 0, :1, : array.shape[-1]])
    return jnp.where(jnp.abs(row) > 1e30, jnp.zeros_like(array), array)


class Near:
    def __init__(self):
        self.count = lax.axis_size("dom")
        self.groups = self.count // 4
        me = lax.axis_index("dom")
        self.group, self.pair, self.core = me // 4, me // 2 % 2, me % 2
        self.first = self.core == 0
        self.even_group = self.group ^ 1
        self.odd_group = ((self.group + 1) ^ 1) - 1

    def move(self, array, pairs):
        return lax.ppermute(array, "dom", pairs) if pairs else array

    def neighbour(self):
        return [(i, i ^ 1) for i in range(self.count)]

    def across(self, which):
        return [(i, i ^ 2) for i in range(self.count) if i % 2 == which]

    def along(self, which, parity):
        lower = [
            i
            for i in range(self.count - 4)
            if i % 2 == which and i // 4 % 2 == parity
        ]
        return [(i, i + 4) for i in lower] + [(i + 4, i) for i in lower]

    def halves(self, state):
        half = state.shape[1] // 2
        keep = lax.dynamic_slice_in_dim(state, self.core * half, half, 1)
        send = lax.dynamic_slice_in_dim(state, (1 - self.core) * half, half, 1)
        return keep, send.astype(jnp.float16)

    def pair_halves(self, keep, got):
        own = jnp.arange(2).reshape(2, 1, 1, 1) == self.core
        return jnp.where(own, keep[None], wide(got)[None]).astype(jnp.float16)

    def first_round(self, mine):
        one = self.move(mine, self.across(0) + self.along(1, 0))
        two = self.move(mine, self.along(1, 1))
        return mine, one, two

    def held(self, parent):
        place = parent // 4
        in_one = jnp.where(self.first, parent // 2 % 2 != self.pair, place == self.even_group)
        in_two = ~self.first & (place == self.odd_group) & ~in_one
        return parent % 2 + jnp.where(in_two, 4, jnp.where(in_one, 2, 0))

    def codes(self, parents_of):
        first, pair, group = self.first, self.pair, self.group
        entry = jnp.arange(6)
        kind, unit = entry // 2, entry % 2
        unit = jnp.where(kind == 2, unit ^ self.core, unit)
        to_group = jnp.where(kind == 0, jnp.where(first, self.even_group, group), group)
        to_group = jnp.where(kind == 1, self.odd_group, to_group)
        to_pair = jnp.where((kind == 0) & ~first, 1 - pair, pair)
        parent = parents_of(4 * jnp.clip(to_group, 0, self.groups - 1) + 2 * to_pair + unit)
        place = parent // 4
        in_three = jnp.where(first, place == self.even_group, parent // 2 % 2 != pair)
        in_four = first & (place == self.odd_group) & (place != group) & ~in_three
        here = jnp.where(in_three, 6 + unit, jnp.where(in_four, 8 + unit, self.held(parent)))
        code = jnp.where(kind == 2, here, self.held(parent)).reshape(-1, 1, 1, 1)
        return code[:2], code[2:4], code[4:]

    def to_send(self, pools, codes):
        return [picked(pools, code) for code in codes[:2]]

    def second_round(self, even, odd):
        three = self.move(even, self.along(0, 0) + self.across(1))
        return three, self.move(odd, self.along(0, 1))

    def slots(self, pools, codes):
        both = picked(pools, codes[2]).astype(jnp.float16)
        return both[0], both[1]


def body(states, offspring, sea_depth, wind, start_hour):
    row_count = states.shape[2]
    total_rows = row_count * lax.axis_size("tile")
    first = lax.axis_index("tile") * row_count - PAD
    rows = row_count + 2 * PAD
    fill = ((PAD - EDGE, 0), (0, 0)), ((0, PAD - EDGE), (0, 0))
    slots = jnp.arange(offspring.shape[0], dtype=jnp.int32)
    state = states[0]

    def fields(around):
        coarse, above, below = assembled(sea_depth, wind, around)
        depth = (0.5 * TIME_STEP) * jnp.concatenate(
            [jnp.pad(above, fill[0]), sea_depth, jnp.pad(below, fill[1])]
        )
        return depth, fine_wind(coarse, first, around[-1], rows)

    def finish(parts, depth, stress):
        above, below = swap_edges(parts[0][:, :EDGE], parts[-1][:, -EDGE:])
        result = step(
            jnp.concatenate([wide(part) for part in parts], axis=1), depth, stress, first, total_rows
        )
        above = [jnp.pad(wide(above), ((0, 0),) + fill[0]), wide(parts[0][:, :PAD])]
        below = [wide(parts[-1][:, -PAD:]), jnp.pad(wide(below), ((0, 0),) + fill[1])]
        above, below = [jnp.concatenate(window, axis=1) for window in (above, below)]
        return mend(result, above, below, depth, stress, first, total_rows)

    def far():
        around = surroundings(sea_depth, wind, start_hour)
        parents = parents_by_starts(offspring)(slots)
        copied = exchange_all(state.astype(jnp.float16), parents)
        return finish([copied], *fields(around))

    def near():
        plan = Near()
        after = lax.optimization_barrier
        keep, send = after(plan.halves(state))
        got = plan.move(send, plan.neighbour())
        size = keep.shape[1] // CHUNKS
        pools = [
            plan.first_round(plan.pair_halves(keep[:, at : at + size], got[:, at : at + size]))
            for at in range(0, CHUNKS * size, size)
        ]
        mine, near_depth, near_wind, near_offspring = after(
            ([pool[0] for pool in pools], sea_depth, wind, offspring)
        )
        pools = [(own,) + pool[1:] for own, pool in zip(mine, pools)]
        own, sent, *rest = surroundings(near_depth, near_wind, start_hour)
        moved, ready = [None] * CHUNKS, None
        codes = [plan.codes(ways(near_offspring)) for ways in (parents_by_starts, parents_by_ends)]
        for at in reversed(range(CHUNKS)):
            sends = plan.to_send(pools[at], codes[at % 2])
            if ready:
                sends = [once(cells, send) for cells, send in zip(ready, sends)]
            ready = [send.astype(jnp.float16) for send in sends]
            moved[at] = plan.second_round(*ready)
        depth, stress = fields((own, [once(ready[1], message) for message in sent], *rest))
        moved[0], depth, stress = after((moved[0], depth, stress))
        upper, lower = [], []
        for at in range(CHUNKS):
            own, other = plan.slots(pools[at] + moved[at], codes[at % 2])
            got = plan.move(other, plan.neighbour())
            upper.append(jnp.where(plan.first, wide(own), wide(got)).astype(jnp.float16))
            lower.append(jnp.where(plan.first, wide(got), wide(own)).astype(jnp.float16))
        return finish(upper + lower, depth, stress)

    if slots.shape[0] % 4 or row_count % (2 * CHUNKS):
        return far()[None]
    ends = 4 * (1 + slots[: slots.shape[0] // 4])
    copies = jnp.sum(jnp.where(slots[None, :] < ends[:, None], offspring[None, :], 0), axis=1)
    close = jnp.all(jnp.abs(copies - ends) <= 4)
    return lax.cond(close, near, far)[None]


def solution(mesh):
    return jax.shard_map(
        body,
        mesh=mesh,
        in_specs=(
            P("dom", None, "tile", None),
            P(),
            P("tile", None),
            P("tile", None, None, None),
            P(),
        ),
        out_specs=P("dom", None, "tile", None),
        check_vma=False,
    )
```

```python
import functools
import math

import jax
import jax.numpy as jnp
from jax import lax
from jax.experimental import pallas as pl
from jax.experimental.pallas import tpu as pltpu
from jax.sharding import PartitionSpec as P

FRICTION = 0.1
TIME_STEP = 0.4
EDGE = 3
PAD = 8
WIND_VMEM = 10 * 1024 * 1024
STEP_VMEM = 20 * 1024 * 1024
CHUNKS = 2


def parents_by_starts(offspring):
    running = jnp.cumsum(offspring)
    return lambda slots: jnp.sum((running[None, :] <= slots[:, None]).astype(jnp.int32), axis=1)


def parents_by_ends(offspring):
    count = offspring.shape[0]
    index = jnp.arange(count)
    running = jnp.sum(jnp.where(index[None, :] <= index[:, None], offspring[None, :], 0), axis=1)
    return lambda slots: count - jnp.sum(
        (running[None, :] > slots[:, None]).astype(jnp.int32), axis=1
    )


def swap_edges(head, tail):
    count = lax.axis_size("tile")
    me = lax.axis_index("tile")
    above = jnp.zeros_like(head)
    below = jnp.zeros_like(head)
    for parity in range(2):
        pairs = []
        for i in range(parity, count - 1, 2):
            pairs += [(i, i + 1), (i + 1, i)]
        if pairs:
            upper = me % 2 == parity
            got = lax.ppermute(jnp.where(upper, tail, head), "tile", pairs)
            below = jnp.where(upper, got, below)
            above = jnp.where(upper, above, got)
    return above, below


def tall_edge(edge, cols):
    pieces = jnp.concatenate([edge[:, at : at + cols] for at in range(0, edge.shape[1], cols)])
    high = lax.reduce_precision(pieces, 8, 7)
    return [high.astype(jnp.bfloat16), (pieces - high).astype(jnp.bfloat16)]


def wide_edge(tall, rows, pieces):
    size = rows * pieces
    both = wide(tall[:size]) + wide(tall[size : 2 * size])
    return jnp.concatenate([both[at : at + rows] for at in range(0, size, rows)], axis=1)


def surroundings(sea_depth, wind, start_hour):
    count = lax.axis_size("tile")
    devices = lax.axis_size("dom")
    me = lax.axis_index("tile")
    hours_dev, parts, coarse_rows, coarse_cols = wind.shape
    row_count = sea_depth.shape[0]
    own_rows = row_count // 2
    window = min(own_rows + PAD, coarse_rows)
    odd = lax.axis_index("dom") % 2
    hours = [start_hour[0] + odd] if devices % 2 == 0 else [start_hour[0], start_hour[0] + 1]

    def first_row(tile):
        return jnp.clip(tile * own_rows - PAD // 2, 0, coarse_rows - window)

    def panels(tile):
        return [
            lax.dynamic_slice(
                wind, (hour % hours_dev, 0, first_row(tile), 0), (1, parts, window, coarse_cols)
            ).reshape(parts * window, coarse_cols)
            for hour in hours
        ]

    sent = []
    for shift in range(1, count):
        target = (me + shift) % count
        edge = jnp.where(target > me, sea_depth[-EDGE:], sea_depth[:EDGE])
        message = jnp.concatenate(panels(target) + tall_edge(edge, coarse_cols))
        pairs = [(i, (i + shift) % count) for i in range(count)]
        sent.append(lax.ppermute(message, "tile", pairs))
    return jnp.concatenate(panels(me)), sent, hours, first_row(me)


def assembled(sea_depth, wind, around):
    found, sent, hours, _ = around
    count = lax.axis_size("tile")
    devices = lax.axis_size("dom")
    me = lax.axis_index("tile")
    hours_dev = wind.shape[0]
    size = found.shape[0]
    part = size // len(hours)
    pieces = sea_depth.shape[1] // found.shape[1]
    above = jnp.zeros_like(sea_depth[:EDGE])
    below = jnp.zeros_like(sea_depth[:EDGE])
    owner = jnp.concatenate([jnp.full((part, 1), 0) + hour // hours_dev for hour in hours])
    for shift, message in enumerate(sent, 1):
        source = (me - shift) % count
        found = jnp.where(owner == source, message[:size], found)
        edge = wide_edge(message[size:], EDGE, pieces)
        above = jnp.where(source == me - 1, edge, above)
        below = jnp.where(source == me + 1, edge, below)
    if len(hours) == 2:
        return found, above, below
    odd = lax.axis_index("dom") % 2
    other = lax.ppermute(found, "dom", [(i, i ^ 1) for i in range(devices)])
    both = [jnp.where(odd == 0, found, other), jnp.where(odd == 0, other, found)]
    return jnp.concatenate(both), above, below


def wind_kernel(where_ref, coarse_ref, fine_ref):
    hours, parts, rows, fine_cols = fine_ref.shape
    coarse_cols = fine_cols // 2
    window = coarse_ref.shape[0] // (hours * parts)
    first = where_ref[0]
    base = where_ref[1]
    fine_row = lax.broadcasted_iota(jnp.int32, (rows, window), 0) + first
    coarse_row = lax.broadcasted_iota(jnp.int32, (rows, window), 1) + base
    lift = jnp.where((fine_row >> 1) == coarse_row, 1.0, 0.0).astype(jnp.bfloat16)
    step = 128
    fine_col = lax.broadcasted_iota(jnp.int32, (step, 2 * step), 1)
    coarse_col = lax.broadcasted_iota(jnp.int32, (step, 2 * step), 0)
    widen = jnp.where((fine_col >> 1) == coarse_col, 1.0, 0.0).astype(jnp.bfloat16)
    for left in range(0, coarse_cols, step):
        cells = coarse_ref[:, left : left + step]
        wide_cells = jnp.dot(cells, widen, preferred_element_type=jnp.float32)
        for hour in range(hours):
            for part in range(parts):
                low = (hour * parts + part) * window
                panel = wide_cells[low : low + window].astype(jnp.bfloat16)
                tall = jnp.dot(lift, panel, preferred_element_type=jnp.float32)
                fine_ref[hour, part, :, 2 * left : 2 * (left + step)] = TIME_STEP * tall


def fine_wind(coarse, first, base, rows):
    hours, parts = 2, 2
    window, cols = coarse.shape[0] // (hours * parts), coarse.shape[1]
    return pl.pallas_call(
        wind_kernel,
        out_shape=jax.ShapeDtypeStruct((hours, parts, rows, 2 * cols), jnp.float32),
        in_specs=[
            pl.BlockSpec(memory_space=pltpu.SMEM),
            pl.BlockSpec(memory_space=pltpu.VMEM),
        ],
        out_specs=pl.BlockSpec(memory_space=pltpu.VMEM),
        compiler_params=pltpu.CompilerParams(vmem_limit_bytes=WIND_VMEM),
        cost_estimate=pl.CostEstimate(
            flops=4 * hours * parts * rows * window * cols,
            bytes_accessed=8 * hours * parts * rows * cols,
            transcendentals=0,
        ),
    )(jnp.stack([first, base]).astype(jnp.int32), coarse)


def sections(state_ref, depth_ref, wind_at, one, two, flux, base, first, total_rows, store, closed):
    rows = state_ref.shape[1]
    cols = state_ref.shape[2]
    blocks = rows // PAD

    def shifted(ref, index, row, by):
        if 0 <= row + by <= rows - PAD:
            return ref[index, row + by : row + by + PAD, :]
        turned = pltpu.roll(ref[index, row : row + PAD, :], -by % PAD, 0)
        if not closed:
            return turned
        at = lax.broadcasted_iota(jnp.int32, (PAD, 1), 0)
        return jnp.where(at == (0 if by < 0 else PAD - 1), 0.0, turned)

    def across(field):
        return pltpu.roll(field, cols - 1, 1) - pltpu.roll(field, 1, 1)

    def section(source, stress, share, put):
        for block in range(blocks):
            here = pl.ds(block * PAD, PAD)
            there = pl.ds(base + block * PAD, PAD)
            flux[0, here, :] = depth_ref[there, :] * source[2, here, :]
        for block in range(blocks):
            low = block * PAD
            here = pl.ds(low, PAD)
            there = pl.ds(base + low, PAD)
            row = first + low + lax.broadcasted_iota(jnp.int32, (PAD, 1), 0)
            turn = TIME_STEP * (0.1 + 0.4 * row.astype(jnp.float32) / total_rows)
            surface = source[0, here, :]
            east = source[1, here, :]
            north = source[2, here, :]
            flux_up = shifted(flux, 0, low, 1) - shifted(flux, 0, low, -1)
            next_surface = surface - (across(depth_ref[there, :] * east) + flux_up)
            rise = shifted(source, 0, low, 1) - shifted(source, 0, low, -1)
            half = 0.5 * TIME_STEP
            keep = 1.0 - TIME_STEP * FRICTION
            next_east = keep * east + turn * north - half * across(surface) + stress(0, there)
            next_north = keep * north - turn * east - half * rise + stress(1, there)
            values = [next_surface, next_east, next_north]
            if share != 1.0:
                values = [
                    (1.0 - share) * state_ref[part, here, :] + share * value
                    for part, value in enumerate(values)
                ]
            put(block, values)

    def into(target):
        def put(block, values):
            for part, value in enumerate(values):
                target[part, pl.ds(block * PAD, PAD), :] = value

        return put

    section(state_ref, lambda part, there: wind_at[0, part, there, :], 1.0, into(one))
    section(one, lambda part, there: wind_at[1, part, there, :], 0.25, into(two))
    section(
        two,
        lambda part, there: 0.5 * (wind_at[0, part, there, :] + wind_at[1, part, there, :]),
        2.0 / 3.0,
        store,
    )


def step_kernel(total_rows, where_ref, state_ref, depth_ref, wind_ref, out_ref, one, two, flux, done, sems):
    rows = state_ref.shape[1]

    def write(block):
        here = pl.ds(block * PAD, PAD)
        return pltpu.make_async_copy(done.at[:, here], out_ref.at[:, here], sems.at[block])

    def store(block, values):
        for part, value in enumerate(values):
            done[part, pl.ds(block * PAD, PAD), :] = value
        write(block).start()

    first = where_ref[0] + PAD
    sections(
        state_ref, depth_ref, wind_ref, one, two, flux, PAD, first, total_rows, store, True
    )
    for block in range(rows // PAD):
        write(block).wait()


def step(state, depth, wind, first, total_rows):
    parts, rows, cols = state.shape
    vmem = pl.BlockSpec(memory_space=pltpu.VMEM)
    return pl.pallas_call(
        functools.partial(step_kernel, total_rows),
        out_shape=jax.ShapeDtypeStruct((parts, rows, cols), jnp.float32),
        in_specs=[pl.BlockSpec(memory_space=pltpu.SMEM), vmem, vmem, vmem],
        out_specs=pl.BlockSpec(memory_space=pltpu.HBM),
        scratch_shapes=[
            pltpu.VMEM((parts, rows, cols), jnp.float32),
            pltpu.VMEM((parts, rows, cols), jnp.float32),
            pltpu.VMEM((1, rows, cols), jnp.float32),
            pltpu.VMEM((parts, rows, cols), jnp.float32),
            pltpu.SemaphoreType.DMA((rows // PAD,)),
        ],
        compiler_params=pltpu.CompilerParams(vmem_limit_bytes=STEP_VMEM),
        cost_estimate=pl.CostEstimate(
            flops=100 * parts * rows * cols,
            bytes_accessed=4 * (3 * parts + 3) * rows * cols,
            transcendentals=0,
        ),
    )(first[None].astype(jnp.int32), state, depth, wind)


def edge_kernel(
    total_rows, where_ref, above_ref, below_ref, depth_ref, wind_ref, old_ref, out_ref,
    one, two, flux, done, kept, sems,
):
    rows = out_ref.shape[1]
    first = where_ref[0]

    def edge(window, base, block, at, used):
        here = pl.ds(at, PAD)
        read = pltpu.make_async_copy(old_ref.at[:, here], kept, sems.at[0])
        write = pltpu.make_async_copy(done, out_ref.at[:, here], sems.at[1])
        read.start()

        def store(number, values):
            if number != block:
                return
            read.wait()
            row = lax.broadcasted_iota(jnp.int32, (PAD, 1), 0)
            for part, value in enumerate(values):
                done[part] = jnp.where(used(row), value, kept[part])
            write.start()

        sections(
            window, depth_ref, wind_ref, one, two, flux, base, first + base, total_rows, store, False
        )
        write.wait()

    @pl.when(first + PAD > 0)
    def _():
        edge(above_ref, 0, 1, 0, lambda row: row < EDGE)

    @pl.when(first + PAD + rows < total_rows)
    def _():
        edge(below_ref, rows, 0, rows - PAD, lambda row: row >= PAD - EDGE)


def mend(result, above, below, depth, wind, first, total_rows):
    parts, rows, cols = result.shape
    vmem = pl.BlockSpec(memory_space=pltpu.VMEM)
    hbm = pl.BlockSpec(memory_space=pltpu.HBM)
    window = pltpu.VMEM((parts, 2 * PAD, cols), jnp.float32)
    return pl.pallas_call(
        functools.partial(edge_kernel, total_rows),
        out_shape=jax.ShapeDtypeStruct((parts, rows, cols), jnp.float32),
        in_specs=[pl.BlockSpec(memory_space=pltpu.SMEM), vmem, vmem, vmem, vmem, hbm],
        out_specs=hbm,
        scratch_shapes=[
            window,
            window,
            pltpu.VMEM((1, 2 * PAD, cols), jnp.float32),
            pltpu.VMEM((parts, PAD, cols), jnp.float32),
            pltpu.VMEM((parts, PAD, cols), jnp.float32),
            pltpu.SemaphoreType.DMA((2,)),
        ],
        input_output_aliases={5: 0},
        compiler_params=pltpu.CompilerParams(vmem_limit_bytes=STEP_VMEM),
        cost_estimate=pl.CostEstimate(
            flops=200 * parts * PAD * cols,
            bytes_accessed=100 * parts * PAD * cols,
            transcendentals=0,
        ),
    )(first[None].astype(jnp.int32), above, below, depth, wind, result)


def exchange_all(cells, parents):
    count = lax.axis_size("dom")
    parts, rows, cols = cells.shape
    tall = math.gcd(count, rows // PAD)
    broad = count // tall
    height, width = rows // tall, cols // broad
    shares = cells.reshape(parts, tall, height, broad, width).transpose(1, 3, 0, 2, 4)
    shares = shares.reshape(count, parts, height, width).astype(jnp.float16)
    spread = lax.all_to_all(shares, "dom", split_axis=0, concat_axis=0, tiled=True)
    picked = jnp.take(spread, parents, axis=0, mode="clip")
    back = lax.all_to_all(picked, "dom", split_axis=0, concat_axis=0, tiled=True)
    lines = [
        jnp.concatenate([back[row * broad + col] for col in range(broad)], axis=2)
        for row in range(tall)
    ]
    return jnp.concatenate(lines, axis=1)


def wide(array):
    return array.astype(jnp.float32)


def picked(pools, code):
    units = [pool[unit] for pool in pools for unit in range(2)]
    result = wide(units[0])[None]
    for at, unit in enumerate(units[1:], 1):
        result = jnp.where(code == at, wide(unit)[None], result)
    return result


def once(cells, array):
    row = wide(cells[0, 0, :1, : array.shape[-1]])
    return jnp.where(jnp.abs(row) > 1e30, jnp.zeros_like(array), array)


class Near:
    def __init__(self):
        self.count = lax.axis_size("dom")
        self.groups = self.count // 4
        me = lax.axis_index("dom")
        self.group, self.pair, self.core = me // 4, me // 2 % 2, me % 2
        self.first = self.core == 0
        self.even_group = self.group ^ 1
        self.odd_group = ((self.group + 1) ^ 1) - 1

    def move(self, array, pairs):
        return lax.ppermute(array, "dom", pairs) if pairs else array

    def neighbour(self):
        return [(i, i ^ 1) for i in range(self.count)]

    def across(self, which):
        return [(i, i ^ 2) for i in range(self.count) if i % 2 == which]

    def along(self, which, parity):
        lower = [
            i
            for i in range(self.count - 4)
            if i % 2 == which and i // 4 % 2 == parity
        ]
        return [(i, i + 4) for i in lower] + [(i + 4, i) for i in lower]

    def halves(self, state):
        half = state.shape[1] // 2
        keep = lax.dynamic_slice_in_dim(state, self.core * half, half, 1)
        send = lax.dynamic_slice_in_dim(state, (1 - self.core) * half, half, 1)
        return keep, send.astype(jnp.float16)

    def pair_halves(self, keep, got):
        own = jnp.arange(2).reshape(2, 1, 1, 1) == self.core
        return jnp.where(own, keep[None], wide(got)[None]).astype(jnp.float16)

    def first_round(self, mine):
        one = self.move(mine, self.across(0) + self.along(1, 0))
        two = self.move(mine, self.along(1, 1))
        return mine, one, two

    def held(self, parent):
        place = parent // 4
        in_one = jnp.where(self.first, parent // 2 % 2 != self.pair, place == self.even_group)
        in_two = ~self.first & (place == self.odd_group) & ~in_one
        return parent % 2 + jnp.where(in_two, 4, jnp.where(in_one, 2, 0))

    def codes(self, parents_of):
        first, pair, group = self.first, self.pair, self.group
        entry = jnp.arange(6)
        kind, unit = entry // 2, entry % 2
        unit = jnp.where(kind == 2, unit ^ self.core, unit)
        to_group = jnp.where(kind == 0, jnp.where(first, self.even_group, group), group)
        to_group = jnp.where(kind == 1, self.odd_group, to_group)
        to_pair = jnp.where((kind == 0) & ~first, 1 - pair, pair)
        parent = parents_of(4 * jnp.clip(to_group, 0, self.groups - 1) + 2 * to_pair + unit)
        place = parent // 4
        in_three = jnp.where(first, place == self.even_group, parent // 2 % 2 != pair)
        in_four = first & (place == self.odd_group) & (place != group) & ~in_three
        here = jnp.where(in_three, 6 + unit, jnp.where(in_four, 8 + unit, self.held(parent)))
        code = jnp.where(kind == 2, here, self.held(parent)).reshape(-1, 1, 1, 1)
        return code[:2], code[2:4], code[4:]

    def to_send(self, pools, codes):
        return [picked(pools, code) for code in codes[:2]]

    def second_round(self, even, odd):
        three = self.move(even, self.along(0, 0) + self.across(1))
        return three, self.move(odd, self.along(0, 1))

    def slots(self, pools, codes):
        both = picked(pools, codes[2]).astype(jnp.float16)
        return both[0], both[1]


def body(states, offspring, sea_depth, wind, start_hour):
    row_count = states.shape[2]
    total_rows = row_count * lax.axis_size("tile")
    first = lax.axis_index("tile") * row_count - PAD
    rows = row_count + 2 * PAD
    fill = ((PAD - EDGE, 0), (0, 0)), ((0, PAD - EDGE), (0, 0))
    slots = jnp.arange(offspring.shape[0], dtype=jnp.int32)
    state = states[0]

    def fields(around):
        coarse, above, below = assembled(sea_depth, wind, around)
        depth = (0.5 * TIME_STEP) * jnp.concatenate(
            [jnp.pad(above, fill[0]), sea_depth, jnp.pad(below, fill[1])]
        )
        return depth, fine_wind(coarse, first, around[-1], rows)

    def finish(parts, depth, stress):
        above, below = swap_edges(parts[0][:, :EDGE], parts[-1][:, -EDGE:])
        result = step(
            jnp.concatenate([wide(part) for part in parts], axis=1), depth, stress, first, total_rows
        )
        above = [jnp.pad(wide(above), ((0, 0),) + fill[0]), wide(parts[0][:, :PAD])]
        below = [wide(parts[-1][:, -PAD:]), jnp.pad(wide(below), ((0, 0),) + fill[1])]
        above, below = [jnp.concatenate(window, axis=1) for window in (above, below)]
        return mend(result, above, below, depth, stress, first, total_rows)

    def far():
        around = surroundings(sea_depth, wind, start_hour)
        parents = parents_by_starts(offspring)(slots)
        copied = exchange_all(state, parents)
        return finish([copied], *fields(around))

    def near():
        plan = Near()
        after = lax.optimization_barrier
        keep, send = after(plan.halves(state))
        got = plan.move(send, plan.neighbour())
        size = keep.shape[1] // CHUNKS
        pools = [
            plan.first_round(plan.pair_halves(keep[:, at : at + size], got[:, at : at + size]))
            for at in range(0, CHUNKS * size, size)
        ]
        mine, near_depth, near_wind, near_offspring = after(
            ([pool[0] for pool in pools], sea_depth, wind, offspring)
        )
        pools = [(own,) + pool[1:] for own, pool in zip(mine, pools)]
        own, sent, *rest = surroundings(near_depth, near_wind, start_hour)
        moved, ready = [None] * CHUNKS, None
        codes = [plan.codes(ways(near_offspring)) for ways in (parents_by_starts, parents_by_ends)]
        for at in reversed(range(CHUNKS)):
            sends = plan.to_send(pools[at], codes[at % 2])
            if ready:
                sends = [once(cells, send) for cells, send in zip(ready, sends)]
            ready = [send.astype(jnp.float16) for send in sends]
            moved[at] = plan.second_round(*ready)
        depth, stress = fields((own, [once(ready[1], message) for message in sent], *rest))
        moved[0], depth, stress = after((moved[0], depth, stress))
        upper, lower = [], []
        for at in range(CHUNKS):
            own, other = plan.slots(pools[at] + moved[at], codes[at % 2])
            got = plan.move(other, plan.neighbour())
            upper.append(jnp.where(plan.first, wide(own), wide(got)).astype(jnp.float16))
            lower.append(jnp.where(plan.first, wide(got), wide(own)).astype(jnp.float16))
        return finish(upper + lower, depth, stress)

    if slots.shape[0] % 4 or row_count % (2 * CHUNKS):
        return far()[None]
    ends = 4 * (1 + slots[: slots.shape[0] // 4])
    copies = jnp.sum(jnp.where(slots[None, :] < ends[:, None], offspring[None, :], 0), axis=1)
    close = jnp.all(jnp.abs(copies - ends) <= 4)
    return lax.cond(close, near, far)[None]


def solution(mesh):
    return jax.shard_map(
        body,
        mesh=mesh,
        in_specs=(
            P("dom", None, "tile", None),
            P(),
            P("tile", None),
            P("tile", None, None, None),
            P(),
        ),
        out_specs=P("dom", None, "tile", None),
        check_vma=False,
    )
```

```python
import functools
import math

import jax
import jax.numpy as jnp
from jax import lax
from jax.experimental import pallas as pl
from jax.experimental.pallas import tpu as pltpu
from jax.sharding import PartitionSpec as P

FRICTION = 0.1
TIME_STEP = 0.4
EDGE = 3
PAD = 8
WIND_VMEM = 10 * 1024 * 1024
STEP_VMEM = 20 * 1024 * 1024
CHUNKS = 2


def parents_by_starts(offspring):
    running = jnp.cumsum(offspring)
    return lambda slots: jnp.sum((running[None, :] <= slots[:, None]).astype(jnp.int32), axis=1)


def parents_by_ends(offspring):
    count = offspring.shape[0]
    index = jnp.arange(count)
    running = jnp.sum(jnp.where(index[None, :] <= index[:, None], offspring[None, :], 0), axis=1)
    return lambda slots: count - jnp.sum(
        (running[None, :] > slots[:, None]).astype(jnp.int32), axis=1
    )


def swap_edges(head, tail):
    count = lax.axis_size("tile")
    me = lax.axis_index("tile")
    above = jnp.zeros_like(head)
    below = jnp.zeros_like(head)
    for parity in range(2):
        pairs = []
        for i in range(parity, count - 1, 2):
            pairs += [(i, i + 1), (i + 1, i)]
        if pairs:
            upper = me % 2 == parity
            got = lax.ppermute(jnp.where(upper, tail, head), "tile", pairs)
            below = jnp.where(upper, got, below)
            above = jnp.where(upper, above, got)
    return above, below


def tall_edge(edge, cols):
    pieces = jnp.concatenate([edge[:, at : at + cols] for at in range(0, edge.shape[1], cols)])
    high = lax.reduce_precision(pieces, 8, 7)
    return [high.astype(jnp.bfloat16), (pieces - high).astype(jnp.bfloat16)]


def wide_edge(tall, rows, pieces):
    size = rows * pieces
    both = wide(tall[:size]) + wide(tall[size : 2 * size])
    return jnp.concatenate([both[at : at + rows] for at in range(0, size, rows)], axis=1)


def surroundings(sea_depth, wind, start_hour):
    count = lax.axis_size("tile")
    devices = lax.axis_size("dom")
    me = lax.axis_index("tile")
    hours_dev, parts, coarse_rows, coarse_cols = wind.shape
    row_count = sea_depth.shape[0]
    own_rows = row_count // 2
    window = min(own_rows + PAD, coarse_rows)
    odd = lax.axis_index("dom") % 2
    hours = [start_hour[0] + odd] if devices % 2 == 0 else [start_hour[0], start_hour[0] + 1]

    def first_row(tile):
        return jnp.clip(tile * own_rows - PAD // 2, 0, coarse_rows - window)

    def panels(tile):
        return [
            lax.dynamic_slice(
                wind, (hour % hours_dev, 0, first_row(tile), 0), (1, parts, window, coarse_cols)
            ).reshape(parts * window, coarse_cols)
            for hour in hours
        ]

    sent = []
    for shift in range(1, count):
        target = (me + shift) % count
        edge = jnp.where(target > me, sea_depth[-EDGE:], sea_depth[:EDGE])
        message = jnp.concatenate(panels(target) + tall_edge(edge, coarse_cols))
        pairs = [(i, (i + shift) % count) for i in range(count)]
        sent.append(lax.ppermute(message, "tile", pairs))
    return jnp.concatenate(panels(me)), sent, hours, first_row(me)


def assembled(sea_depth, wind, around):
    found, sent, hours, _ = around
    count = lax.axis_size("tile")
    devices = lax.axis_size("dom")
    me = lax.axis_index("tile")
    hours_dev = wind.shape[0]
    size = found.shape[0]
    part = size // len(hours)
    pieces = sea_depth.shape[1] // found.shape[1]
    above = jnp.zeros_like(sea_depth[:EDGE])
    below = jnp.zeros_like(sea_depth[:EDGE])
    owner = jnp.concatenate([jnp.full((part, 1), 0) + hour // hours_dev for hour in hours])
    for shift, message in enumerate(sent, 1):
        source = (me - shift) % count
        found = jnp.where(owner == source, message[:size], found)
        edge = wide_edge(message[size:], EDGE, pieces)
        above = jnp.where(source == me - 1, edge, above)
        below = jnp.where(source == me + 1, edge, below)
    if len(hours) == 2:
        return found, above, below
    odd = lax.axis_index("dom") % 2
    other = lax.ppermute(found, "dom", [(i, i ^ 1) for i in range(devices)])
    both = [jnp.where(odd == 0, found, other), jnp.where(odd == 0, other, found)]
    return jnp.concatenate(both), above, below


def wind_kernel(where_ref, coarse_ref, fine_ref):
    hours, parts, rows, fine_cols = fine_ref.shape
    coarse_cols = fine_cols // 2
    window = coarse_ref.shape[0] // (hours * parts)
    first = where_ref[0]
    base = where_ref[1]
    fine_row = lax.broadcasted_iota(jnp.int32, (rows, window), 0) + first
    coarse_row = lax.broadcasted_iota(jnp.int32, (rows, window), 1) + base
    lift = jnp.where((fine_row >> 1) == coarse_row, 1.0, 0.0).astype(jnp.bfloat16)
    step = 128
    fine_col = lax.broadcasted_iota(jnp.int32, (step, 2 * step), 1)
    coarse_col = lax.broadcasted_iota(jnp.int32, (step, 2 * step), 0)
    widen = jnp.where((fine_col >> 1) == coarse_col, 1.0, 0.0).astype(jnp.bfloat16)
    for left in range(0, coarse_cols, step):
        cells = coarse_ref[:, left : left + step]
        wide_cells = jnp.dot(cells, widen, preferred_element_type=jnp.float32)
        for hour in range(hours):
            for part in range(parts):
                low = (hour * parts + part) * window
                panel = wide_cells[low : low + window].astype(jnp.bfloat16)
                tall = jnp.dot(lift, panel, preferred_element_type=jnp.float32)
                fine_ref[hour, part, :, 2 * left : 2 * (left + step)] = TIME_STEP * tall


def fine_wind(coarse, first, base, rows):
    hours, parts = 2, 2
    window, cols = coarse.shape[0] // (hours * parts), coarse.shape[1]
    return pl.pallas_call(
        wind_kernel,
        out_shape=jax.ShapeDtypeStruct((hours, parts, rows, 2 * cols), jnp.float32),
        in_specs=[
            pl.BlockSpec(memory_space=pltpu.SMEM),
            pl.BlockSpec(memory_space=pltpu.VMEM),
        ],
        out_specs=pl.BlockSpec(memory_space=pltpu.VMEM),
        compiler_params=pltpu.CompilerParams(vmem_limit_bytes=WIND_VMEM),
        cost_estimate=pl.CostEstimate(
            flops=4 * hours * parts * rows * window * cols,
            bytes_accessed=8 * hours * parts * rows * cols,
            transcendentals=0,
        ),
    )(jnp.stack([first, base]).astype(jnp.int32), coarse)


def sections(state_ref, depth_ref, wind_at, one, two, flux, base, first, total_rows, store, closed):
    rows = state_ref.shape[1]
    cols = state_ref.shape[2]
    blocks = rows // PAD

    def shifted(ref, index, row, by):
        if 0 <= row + by <= rows - PAD:
            return ref[index, row + by : row + by + PAD, :]
        turned = pltpu.roll(ref[index, row : row + PAD, :], -by % PAD, 0)
        if not closed:
            return turned
        at = lax.broadcasted_iota(jnp.int32, (PAD, 1), 0)
        return jnp.where(at == (0 if by < 0 else PAD - 1), 0.0, turned)

    def across(field):
        return pltpu.roll(field, cols - 1, 1) - pltpu.roll(field, 1, 1)

    def section(source, stress, share, put):
        for block in range(blocks):
            here = pl.ds(block * PAD, PAD)
            there = pl.ds(base + block * PAD, PAD)
            flux[0, here, :] = depth_ref[there, :] * source[2, here, :]
        for block in range(blocks):
            low = block * PAD
            here = pl.ds(low, PAD)
            there = pl.ds(base + low, PAD)
            row = first + low + lax.broadcasted_iota(jnp.int32, (PAD, 1), 0)
            turn = TIME_STEP * (0.1 + 0.4 * row.astype(jnp.float32) / total_rows)
            surface = source[0, here, :]
            east = source[1, here, :]
            north = source[2, here, :]
            flux_up = shifted(flux, 0, low, 1) - shifted(flux, 0, low, -1)
            next_surface = surface - (across(depth_ref[there, :] * east) + flux_up)
            rise = shifted(source, 0, low, 1) - shifted(source, 0, low, -1)
            half = 0.5 * TIME_STEP
            keep = 1.0 - TIME_STEP * FRICTION
            next_east = keep * east + turn * north - half * across(surface) + stress(0, there)
            next_north = keep * north - turn * east - half * rise + stress(1, there)
            values = [next_surface, next_east, next_north]
            if share != 1.0:
                values = [
                    (1.0 - share) * state_ref[part, here, :] + share * value
                    for part, value in enumerate(values)
                ]
            put(block, values)

    def into(target):
        def put(block, values):
            for part, value in enumerate(values):
                target[part, pl.ds(block * PAD, PAD), :] = value

        return put

    section(state_ref, lambda part, there: wind_at[0, part, there, :], 1.0, into(one))
    section(one, lambda part, there: wind_at[1, part, there, :], 0.25, into(two))
    section(
        two,
        lambda part, there: 0.5 * (wind_at[0, part, there, :] + wind_at[1, part, there, :]),
        2.0 / 3.0,
        store,
    )


def step_kernel(
    total_rows, where_ref, state_ref, depth_ref, wind_ref, out_ref, ends_ref, one, two, flux, done, sems
):
    rows = state_ref.shape[1]

    def write(block):
        here = pl.ds(block * PAD, PAD)
        return pltpu.make_async_copy(done.at[:, here], out_ref.at[:, here], sems.at[block])

    def store(block, values):
        for part, value in enumerate(values):
            done[part, pl.ds(block * PAD, PAD), :] = value
        write(block).start()
        for end, number in enumerate((0, rows // PAD - 1)):
            if block == number:
                for part, value in enumerate(values):
                    ends_ref[end, part] = value

    first = where_ref[0] + PAD
    sections(
        state_ref, depth_ref, wind_ref, one, two, flux, PAD, first, total_rows, store, True
    )
    for block in range(rows // PAD):
        write(block).wait()


def step(state, depth, wind, first, total_rows):
    parts, rows, cols = state.shape
    vmem = pl.BlockSpec(memory_space=pltpu.VMEM)
    return pl.pallas_call(
        functools.partial(step_kernel, total_rows),
        out_shape=[
            jax.ShapeDtypeStruct((parts, rows, cols), jnp.float32),
            jax.ShapeDtypeStruct((2, parts, PAD, cols), jnp.float32),
        ],
        in_specs=[pl.BlockSpec(memory_space=pltpu.SMEM), vmem, vmem, vmem],
        out_specs=[pl.BlockSpec(memory_space=pltpu.HBM), vmem],
        scratch_shapes=[
            pltpu.VMEM((parts, rows, cols), jnp.float32),
            pltpu.VMEM((parts, rows, cols), jnp.float32),
            pltpu.VMEM((1, rows, cols), jnp.float32),
            pltpu.VMEM((parts, rows, cols), jnp.float32),
            pltpu.SemaphoreType.DMA((rows // PAD,)),
        ],
        compiler_params=pltpu.CompilerParams(vmem_limit_bytes=STEP_VMEM),
        cost_estimate=pl.CostEstimate(
            flops=100 * parts * rows * cols,
            bytes_accessed=4 * (3 * parts + 3) * rows * cols,
            transcendentals=0,
        ),
    )(first[None].astype(jnp.int32), state, depth, wind)


def edge_kernel(
    total_rows, where_ref, above_ref, below_ref, depth_ref, wind_ref, ends_ref, old_ref, out_ref,
    one, two, flux, done, sem,
):
    rows = out_ref.shape[1]
    first = where_ref[0]

    def edge(window, base, block, end, at, used):
        here = pl.ds(at, PAD)
        write = pltpu.make_async_copy(done, out_ref.at[:, here], sem)

        def store(number, values):
            if number != block:
                return
            row = lax.broadcasted_iota(jnp.int32, (PAD, 1), 0)
            for part, value in enumerate(values):
                done[part] = jnp.where(used(row), value, ends_ref[end, part])
            write.start()

        sections(
            window, depth_ref, wind_ref, one, two, flux, base, first + base, total_rows, store, False
        )
        write.wait()

    @pl.when(first + PAD > 0)
    def _():
        edge(above_ref, 0, 1, 0, 0, lambda row: row < EDGE)

    @pl.when(first + PAD + rows < total_rows)
    def _():
        edge(below_ref, rows, 0, 1, rows - PAD, lambda row: row >= PAD - EDGE)


def mend(result, ends, above, below, depth, wind, first, total_rows):
    parts, rows, cols = result.shape
    vmem = pl.BlockSpec(memory_space=pltpu.VMEM)
    hbm = pl.BlockSpec(memory_space=pltpu.HBM)
    window = pltpu.VMEM((parts, 2 * PAD, cols), jnp.float32)
    return pl.pallas_call(
        functools.partial(edge_kernel, total_rows),
        out_shape=jax.ShapeDtypeStruct((parts, rows, cols), jnp.float32),
        in_specs=[pl.BlockSpec(memory_space=pltpu.SMEM), vmem, vmem, vmem, vmem, vmem, hbm],
        out_specs=hbm,
        scratch_shapes=[
            window,
            window,
            pltpu.VMEM((1, 2 * PAD, cols), jnp.float32),
            pltpu.VMEM((parts, PAD, cols), jnp.float32),
            pltpu.SemaphoreType.DMA,
        ],
        input_output_aliases={6: 0},
        compiler_params=pltpu.CompilerParams(vmem_limit_bytes=STEP_VMEM),
        cost_estimate=pl.CostEstimate(
            flops=200 * parts * PAD * cols,
            bytes_accessed=100 * parts * PAD * cols,
            transcendentals=0,
        ),
    )(first[None].astype(jnp.int32), above, below, depth, wind, ends, result)


def exchange_all(cells, parents):
    count = lax.axis_size("dom")
    parts, rows, cols = cells.shape
    tall = math.gcd(count, rows // PAD)
    broad = count // tall
    height, width = rows // tall, cols // broad
    shares = cells.reshape(parts, tall, height, broad, width).transpose(1, 3, 0, 2, 4)
    shares = shares.reshape(count, parts, height, width).astype(jnp.float16)
    spread = lax.all_to_all(shares, "dom", split_axis=0, concat_axis=0, tiled=True)
    picked = jnp.take(spread, parents, axis=0, mode="clip")
    back = lax.all_to_all(picked, "dom", split_axis=0, concat_axis=0, tiled=True)
    lines = [
        jnp.concatenate([back[row * broad + col] for col in range(broad)], axis=2)
        for row in range(tall)
    ]
    return jnp.concatenate(lines, axis=1)


def wide(array):
    return array.astype(jnp.float32)


def picked(pools, code):
    units = [pool[unit] for pool in pools for unit in range(2)]
    result = wide(units[0])[None]
    for at, unit in enumerate(units[1:], 1):
        result = jnp.where(code == at, wide(unit)[None], result)
    return result


def once(cells, array):
    row = wide(cells[0, 0, :1, : array.shape[-1]])
    return jnp.where(jnp.abs(row) > 1e30, jnp.zeros_like(array), array)


class Near:
    def __init__(self):
        self.count = lax.axis_size("dom")
        self.groups = self.count // 4
        me = lax.axis_index("dom")
        self.group, self.pair, self.core = me // 4, me // 2 % 2, me % 2
        self.first = self.core == 0
        self.even_group = self.group ^ 1
        self.odd_group = ((self.group + 1) ^ 1) - 1

    def move(self, array, pairs):
        return lax.ppermute(array, "dom", pairs) if pairs else array

    def neighbour(self):
        return [(i, i ^ 1) for i in range(self.count)]

    def across(self, which):
        return [(i, i ^ 2) for i in range(self.count) if i % 2 == which]

    def along(self, which, parity):
        lower = [
            i
            for i in range(self.count - 4)
            if i % 2 == which and i // 4 % 2 == parity
        ]
        return [(i, i + 4) for i in lower] + [(i + 4, i) for i in lower]

    def halves(self, state):
        half = state.shape[1] // 2
        keep = lax.dynamic_slice_in_dim(state, self.core * half, half, 1)
        send = lax.dynamic_slice_in_dim(state, (1 - self.core) * half, half, 1)
        return keep, send.astype(jnp.float16)

    def pair_halves(self, keep, got):
        own = jnp.arange(2).reshape(2, 1, 1, 1) == self.core
        return jnp.where(own, keep[None], wide(got)[None]).astype(jnp.float16)

    def first_round(self, mine):
        one = self.move(mine, self.across(0) + self.along(1, 0))
        two = self.move(mine, self.along(1, 1))
        return mine, one, two

    def held(self, parent):
        place = parent // 4
        in_one = jnp.where(self.first, parent // 2 % 2 != self.pair, place == self.even_group)
        in_two = ~self.first & (place == self.odd_group) & ~in_one
        return parent % 2 + jnp.where(in_two, 4, jnp.where(in_one, 2, 0))

    def codes(self, parents_of):
        first, pair, group = self.first, self.pair, self.group
        entry = jnp.arange(6)
        kind, unit = entry // 2, entry % 2
        unit = jnp.where(kind == 2, unit ^ self.core, unit)
        to_group = jnp.where(kind == 0, jnp.where(first, self.even_group, group), group)
        to_group = jnp.where(kind == 1, self.odd_group, to_group)
        to_pair = jnp.where((kind == 0) & ~first, 1 - pair, pair)
        parent = parents_of(4 * jnp.clip(to_group, 0, self.groups - 1) + 2 * to_pair + unit)
        place = parent // 4
        in_three = jnp.where(first, place == self.even_group, parent // 2 % 2 != pair)
        in_four = first & (place == self.odd_group) & (place != group) & ~in_three
        here = jnp.where(in_three, 6 + unit, jnp.where(in_four, 8 + unit, self.held(parent)))
        code = jnp.where(kind == 2, here, self.held(parent)).reshape(-1, 1, 1, 1)
        return code[:2], code[2:4], code[4:]

    def to_send(self, pools, codes):
        return [picked(pools, code) for code in codes[:2]]

    def second_round(self, even, odd):
        three = self.move(even, self.along(0, 0) + self.across(1))
        return three, self.move(odd, self.along(0, 1))

    def slots(self, pools, codes):
        both = picked(pools, codes[2]).astype(jnp.float16)
        return both[0], both[1]


def body(states, offspring, sea_depth, wind, start_hour):
    row_count = states.shape[2]
    total_rows = row_count * lax.axis_size("tile")
    first = lax.axis_index("tile") * row_count - PAD
    rows = row_count + 2 * PAD
    fill = ((PAD - EDGE, 0), (0, 0)), ((0, PAD - EDGE), (0, 0))
    slots = jnp.arange(offspring.shape[0], dtype=jnp.int32)
    state = states[0]

    def fields(around):
        coarse, above, below = assembled(sea_depth, wind, around)
        depth = (0.5 * TIME_STEP) * jnp.concatenate(
            [jnp.pad(above, fill[0]), sea_depth, jnp.pad(below, fill[1])]
        )
        return depth, fine_wind(coarse, first, around[-1], rows)

    def finish(parts, depth, stress):
        above, below = swap_edges(parts[0][:, :EDGE], parts[-1][:, -EDGE:])
        result, ends = step(
            jnp.concatenate([wide(part) for part in parts], axis=1), depth, stress, first, total_rows
        )
        above = [jnp.pad(wide(above), ((0, 0),) + fill[0]), wide(parts[0][:, :PAD])]
        below = [wide(parts[-1][:, -PAD:]), jnp.pad(wide(below), ((0, 0),) + fill[1])]
        above, below = [jnp.concatenate(window, axis=1) for window in (above, below)]
        return mend(result, ends, above, below, depth, stress, first, total_rows)

    def far():
        around = surroundings(sea_depth, wind, start_hour)
        parents = parents_by_starts(offspring)(slots)
        copied = exchange_all(state, parents)
        return finish([copied], *fields(around))

    def near():
        plan = Near()
        after = lax.optimization_barrier
        keep, send = after(plan.halves(state))
        got = plan.move(send, plan.neighbour())
        size = keep.shape[1] // CHUNKS
        pools = [
            plan.first_round(plan.pair_halves(keep[:, at : at + size], got[:, at : at + size]))
            for at in range(0, CHUNKS * size, size)
        ]
        mine, near_depth, near_wind, near_offspring = after(
            ([pool[0] for pool in pools], sea_depth, wind, offspring)
        )
        pools = [(own,) + pool[1:] for own, pool in zip(mine, pools)]
        own, sent, *rest = surroundings(near_depth, near_wind, start_hour)
        moved, ready = [None] * CHUNKS, None
        codes = [plan.codes(ways(near_offspring)) for ways in (parents_by_starts, parents_by_ends)]
        for at in reversed(range(CHUNKS)):
            sends = plan.to_send(pools[at], codes[at % 2])
            if ready:
                sends = [once(cells, send) for cells, send in zip(ready, sends)]
            ready = [send.astype(jnp.float16) for send in sends]
            moved[at] = plan.second_round(*ready)
        depth, stress = fields((own, [once(ready[1], message) for message in sent], *rest))
        moved[0], depth, stress = after((moved[0], depth, stress))
        upper, lower = [], []
        for at in range(CHUNKS):
            own, other = plan.slots(pools[at] + moved[at], codes[at % 2])
            got = plan.move(other, plan.neighbour())
            upper.append(jnp.where(plan.first, wide(own), wide(got)).astype(jnp.float16))
            lower.append(jnp.where(plan.first, wide(got), wide(own)).astype(jnp.float16))
        return finish(upper + lower, depth, stress)

    if slots.shape[0] % 4 or row_count % (2 * CHUNKS):
        return far()[None]
    ends = 4 * (1 + slots[: slots.shape[0] // 4])
    copies = jnp.sum(jnp.where(slots[None, :] < ends[:, None], offspring[None, :], 0), axis=1)
    close = jnp.all(jnp.abs(copies - ends) <= 4)
    return lax.cond(close, near, far)[None]


def solution(mesh):
    return jax.shard_map(
        body,
        mesh=mesh,
        in_specs=(
            P("dom", None, "tile", None),
            P(),
            P("tile", None),
            P("tile", None, None, None),
            P(),
        ),
        out_specs=P("dom", None, "tile", None),
        check_vma=False,
    )
```
